128 devices in a mesh: rows: 16 (over y, x), tensor: 8 (over z, core).
Axes of the slice: x: 4, y: 4, z: 4, core: 2. Of those that a mesh axis runs over, the one named last changes fastest.
Arguments:
- tokens: bfloat16 [16384, 4096], P('rows'), may hold values from -6 to 6
- grid_sizes: int32 [16, 4, 2], replicated, may hold values from 8 to 22, as said below
- owners: int32 [4096, 1], replicated, may hold values from 0 to 15; in each aligned block of 256 rows (0 to 255, 256 to 511, ...) at most 24 rows name the same one
- ln_gain: float32 [4096], replicated, may hold values from 0.5 to 1.5
- ln_bias: float32 [4096], replicated, may hold values from -4 to 4
- w_qkv: bfloat16 [4096, 3, 4096], P('rows', None, 'tensor')
- w_out: bfloat16 [4096, 4096], P('tensor', 'rows'), may hold values from -0.09375 to 0.09375
- layer_scale: float32 [4096], replicated, may hold values from 0.2 to 2
- merge_gain: float32 [4, 4096], replicated, may hold values from 0.5 to 1.5
- merge_bias: float32 [4, 4096], replicated, may hold values from -4 to 4
- w_merge: bfloat16 [4, 4096, 2048], P(None, 'rows', 'tensor'), may hold values from -0.046875 to 0.046875
Outputs:
- received: bfloat16 [6144, 2048], P('rows', 'tensor')
The draws below stay inside these ranges and needn't reach their ends.
Inputs may be any that keep to these rules, and one draw needn't show every extreme that they name: `grid_sizes`: image grids have even sides with 96 to 396 patches, so images hold 101 to 401 tokens; each block's images together hold at most 1024 tokens; in every draw some image has 22 x 18 patches (height 22, width 18) and some has 8 x 12 (height 8, width 12). `owners`: no owner is named by more than 24 of the 256 merged slots of one block.
All inputs are finite; a program needn't handle non-finite values.
Results may differ from the reference program's by a relative error of at most 0.013.
Values may be sent and summed in bfloat16 or wider, within the bound.
A program may use at most 128 MiB of HBM per device.

```python
import math
import jax
import jax.numpy as jnp
import numpy as np
from jax import lax

D = 4096
HEADS = 32
HEAD_DIM = 128
MERGE_OUT = 2048
PREFIX = 5
TOK_DEV = 1024
IMAGES_DEV = 4
MERGED_DEV = 256
SLOTS = 24
TOKENS = 16384
MERGED = 4096
N_ROWS = 16
N_TENSOR = 8


def grid_entries():
    listing = []
    for height in range(8, 23, 2):
        for width in range(8, 23, 2):
            if 96 <= height * width <= 396:
                listing.append((height * width, height, width))
    listing.sort()
    return np.array([[entry[1], entry[2]] for entry in listing], dtype=np.int32)


def draw_grid_sizes(key, part):
    entries = jnp.asarray(grid_entries())
    lengths = PREFIX + entries[:, 0] * entries[:, 1]
    final_entry = entries.shape[0] - 1
    first_key, second_key, third_key = jax.random.split(key, 3)
    big_device = jax.random.randint(first_key, (), 0, N_ROWS)
    small_device = (big_device + 1 + jax.random.randint(second_key, (), 0, N_ROWS - 1)) % N_ROWS

    def per_device(device_key, device_number):
        remaining = jnp.int32(TOK_DEV)
        picked = []
        for slot_number in range(IMAGES_DEV):
            ceiling = remaining - (IMAGES_DEV - 1 - slot_number) * 101
            counted = jnp.sum((lengths <= ceiling).astype(jnp.int32))
            chosen = jax.random.randint(jax.random.fold_in(device_key, slot_number), (), 0, counted)
            if slot_number == 0:
                chosen = jnp.where(device_number == big_device, final_entry, jnp.where(device_number == small_device, 0, chosen))
            remaining = remaining - lengths[chosen]
            picked.append(entries[chosen])
        return jnp.stack(picked)
    device_keys = jax.random.split(third_key, N_ROWS)
    return jax.vmap(per_device)(device_keys, jnp.arange(N_ROWS, dtype=jnp.int32)).astype(jnp.int32)


def draw_w_qkv(key, part):
    weights = jax.random.normal(key, (D, 3, HEADS * HEAD_DIM), jnp.float32) * D ** (-0.5)
    return weights.astype(jnp.bfloat16)


def block_scale(key, extent, shards, smallest, top_value):
    level = 1.0
    for axis_at, blocks in shards:
        steps = jax.random.uniform(jax.random.fold_in(jax.random.fold_in(key, 6), axis_at), (blocks,), jnp.float32, smallest / len(shards), top_value / len(shards))
        level = level * jnp.repeat(jnp.exp(steps), extent[axis_at] // blocks).reshape((-1,) + (1,) * (len(extent) - 1 - axis_at))
    return level


def routed_block(own_key, own, number, rows, amount, top, most, slope):
    order = jax.random.permutation(own_key, amount)
    packed, usual = portions_of(amount, rows * top, most, slope, True), portions_of(amount, rows * top, most, slope, False)
    places = jnp.arange(amount)

    def named(sizes, turn):
        used = int((sizes > 0).sum())
        fixed = max(1, used // 4)
        moved = fixed + (places - fixed + turn * (used - fixed)) % max(1, amount - fixed)
        return jnp.zeros((amount,), jnp.int32).at[order[jnp.where(places < fixed, places, moved)]].set(jnp.asarray(sizes, jnp.int32))

    sizes = jnp.where(number % 4 == 0, named(packed, number // 4), named(usual, number - number // 4 - 1))
    mixed = jax.random.permutation(jax.random.fold_in(own, 3), amount)
    giver, receiver = mixed[0:amount // 2 * 2:2], mixed[1:amount // 2 * 2:2]
    room = jnp.minimum(sizes[giver] - 1, most - sizes[receiver]) // 2
    room = jnp.where((giver == order[0]) | (receiver == order[0]) | (sizes[receiver] == 0), 0, jnp.maximum(room, 0))
    moved = jax.random.randint(jax.random.fold_in(own, 4), (amount // 2,), 0, 1 << 20) % (room + 1)
    sizes = sizes.at[giver].add(-moved).at[receiver].add(moved)
    items = jnp.searchsorted(jnp.cumsum(sizes), jnp.arange(rows * top), side="right").astype(jnp.int32)
    table = items.reshape(top, rows).T
    table = table[jax.random.permutation(jax.random.fold_in(own, 1), rows)]
    turn = jax.random.randint(jax.random.fold_in(own, 2), (rows, 1), 0, top)
    return jnp.take_along_axis(table, (jnp.arange(top)[None, :] + turn) % top, axis=1)


def portions_of(amount, total, bound, lean, full):
    portions = [(1 << 20) // math.isqrt(standing ** lean) + 1 for standing in range(1, amount + 1)]
    largest = bound if full else min(bound, max(-(-total // amount), total * portions[0] // sum(portions)))
    least = 1 if total - largest >= amount - 1 else 0
    given, spare = [largest] + [least] * (amount - 1), total - largest - least * (amount - 1)
    while spare > 0:
        movable = [i for i in range(1, amount) if given[i] < largest] or [i for i in range(1, amount) if given[i] < bound]
        mass, left = sum([portions[i] for i in movable]), spare
        for i in movable:
            more = min(bound - given[i], max(1, left * portions[i] // mass), spare)
            given[i] = given[i] + more
            spare = spare - more
    return np.array(given)


def scatter_about(key, dims, deviation, most, cuts=(), held_as=jnp.bfloat16):
    loudness = block_scale(key, dims, cuts, -0.22, 0.18) if cuts else 1.0
    values = jax.random.normal(key, dims, jnp.float32) * deviation * loudness
    return jnp.minimum(jnp.maximum(values, -most), most).astype(held_as)


def setup_inputs(seed: int = 0) -> dict:
    keys = jax.random.split(jax.random.key(seed), 12)
    tokens = scatter_about(keys[0], (TOKENS, D), 1.0, 6.0, ((0, 16),))
    grid_sizes = draw_grid_sizes(jax.random.fold_in(keys[11], 71), 0)
    owners_keys = jax.random.split(jax.random.fold_in(keys[2], 1), MERGED // MERGED_DEV)
    owners_turns = jax.random.permutation(jax.random.fold_in(keys[2], 3), MERGED // MERGED_DEV)
    owners = jax.vmap(lambda own, number: routed_block(jax.random.fold_in(keys[2], 2), own, number, MERGED_DEV, N_ROWS, 1, SLOTS, 2))(owners_keys, owners_turns).reshape((MERGED, 1))
    ln_gain = jnp.clip(1.0 + 0.1 * jax.random.normal(keys[3], (D,), jnp.float32), 0.5, 1.5)
    ln_bias = scatter_about(keys[4], (D,), 0.3, 4.0, (), jnp.float32)
    w_qkv = draw_w_qkv(jax.random.fold_in(keys[11], 71), 0)
    w_out = scatter_about(keys[6], (HEADS * HEAD_DIM, D), (HEADS * HEAD_DIM) ** -0.5, 0.09375, ((0, 8), (1, 16)))
    layer_scale = jnp.clip(jnp.exp(jax.random.uniform(keys[7], (D,), jnp.float32, math.log(0.2), math.log(2.0))), 0.2, 2.0)
    merge_gain = jnp.clip(1.0 + 0.1 * jax.random.normal(keys[8], (4, D), jnp.float32), 0.5, 1.5)
    merge_bias = scatter_about(keys[9], (4, D), 0.3, 4.0, (), jnp.float32)
    w_merge = scatter_about(keys[10], (4, D, MERGE_OUT), (4 * D) ** -0.5, 0.046875, ((1, 16), (2, 8)))
    return dict(tokens=tokens, grid_sizes=grid_sizes, owners=owners, ln_gain=ln_gain, ln_bias=ln_bias, w_qkv=w_qkv, w_out=w_out, layer_scale=layer_scale, merge_gain=merge_gain, merge_bias=merge_bias, w_merge=w_merge)


def image_layout(device_grid, tok_count, merged_count):
    heights = device_grid[:, 0]
    widths = device_grid[:, 1]
    image_total = device_grid.shape[0]
    lengths = PREFIX + heights * widths
    starts = jnp.cumsum(lengths, dtype=jnp.int32) - lengths
    positions = jnp.arange(tok_count, dtype=jnp.int32)
    inside = ((positions[:, None] >= starts[None, :]) & (positions[:, None] < (starts + lengths)[None, :])).astype(jnp.int32)
    image_ids = jnp.arange(image_total, dtype=jnp.int32)
    occupied = lax.optimization_barrier(jnp.sum(inside, axis=1, dtype=jnp.int32))
    segment = lax.optimization_barrier(jnp.sum(inside * image_ids[None, :], axis=1, dtype=jnp.int32)) + image_total * (1 - occupied)
    local_pos = positions - lax.optimization_barrier(jnp.sum(inside * starts[None, :], axis=1, dtype=jnp.int32))
    width_here = jnp.maximum(lax.optimization_barrier(jnp.sum(inside * widths[None, :], axis=1, dtype=jnp.int32)), 1)
    is_patch = occupied * (local_pos >= PREFIX).astype(jnp.int32)
    flat_patch = jnp.maximum(local_pos - PREFIX, 0) * is_patch
    row_index = flat_patch // width_here
    col_index = flat_patch % width_here
    merged_counts = heights * widths // 4
    merged_starts = jnp.cumsum(merged_counts, dtype=jnp.int32) - merged_counts
    slot_ids = jnp.arange(merged_count, dtype=jnp.int32)
    within = ((slot_ids[:, None] >= merged_starts[None, :]) & (slot_ids[:, None] < (merged_starts + merged_counts)[None, :])).astype(jnp.int32)
    is_live = lax.optimization_barrier(jnp.sum(within, axis=1, dtype=jnp.int32))
    offset_in = slot_ids - lax.optimization_barrier(jnp.sum(within * merged_starts[None, :], axis=1, dtype=jnp.int32))
    image_width = lax.optimization_barrier(jnp.sum(within * widths[None, :], axis=1, dtype=jnp.int32))
    half_width = jnp.maximum(image_width // 2, 1)
    first_patch = lax.optimization_barrier(jnp.sum(within * starts[None, :], axis=1, dtype=jnp.int32)) + PREFIX
    merged_row = offset_in // half_width
    merged_col = offset_in % half_width
    picks = []
    for down in (0, 1):
        for across in (0, 1):
            picks.append(first_patch + (2 * merged_row + down) * image_width + 2 * merged_col + across)
    sources = jnp.stack(picks, axis=1) * is_live[:, None]
    return (segment, row_index, col_index, is_patch, sources, is_live)

def route_slots(owner_dev, is_live, rows_count, slot_count):
    hits = (owner_dev[:, None] == jnp.arange(rows_count, dtype=jnp.int32)[None, :]).astype(jnp.int32) * is_live[:, None]
    before = jnp.cumsum(hits, axis=0, dtype=jnp.int32) - hits
    ranking = lax.optimization_barrier(jnp.sum(before * hits, axis=1, dtype=jnp.int32))
    return jnp.where(is_live > 0, owner_dev * slot_count + ranking, rows_count * slot_count)

def rotate_pairs(values, row_index, col_index, is_patch):
    quarter = values.shape[-1] // 4
    freqs = 100.0 ** (-jnp.arange(quarter, dtype=jnp.float32) / quarter)
    patch_mask = is_patch.astype(jnp.float32)
    pieces_out = []
    for coord, lowest in ((row_index, 0), (col_index, 2 * quarter)):
        angle = (coord.astype(jnp.float32) * patch_mask)[:, None] * freqs[None, :]
        cosine = jnp.cos(angle)[:, None, :]
        sine = jnp.sin(angle)[:, None, :]
        first = values[..., lowest:lowest + quarter]
        second = values[..., lowest + quarter:lowest + 2 * quarter]
        pieces_out.append(first * cosine - second * sine)
        pieces_out.append(second * cosine + first * sine)
    return jnp.concatenate(pieces_out, axis=-1)

def layer_norm(values, gain, bias, axes):
    mean_value = lax.optimization_barrier(jnp.mean(values, axis=axes, keepdims=True))
    centered = values - mean_value
    variance = lax.optimization_barrier(jnp.mean(centered * centered, axis=axes, keepdims=True))
    return centered * lax.rsqrt(variance + 1e-06) * gain + bias

def reference(tokens, grid_sizes, owners, ln_gain, ln_bias, w_qkv, w_out, layer_scale, merge_gain, merge_bias, w_merge):
    width_heads = HEADS * HEAD_DIM
    group_cols = width_heads // N_TENSOR
    slot_count = SLOTS
    all_tokens = tokens.reshape(N_ROWS, TOK_DEV, D)
    all_owners = owners[:, 0].reshape(N_ROWS, MERGED_DEV)

    def per_device(inputs):
        block, device_grid, owner_dev = inputs
        segment, row_index, col_index, is_patch, sources, is_live = image_layout(device_grid, TOK_DEV, MERGED_DEV)
        block_f = block.astype(jnp.float32)
        normed = layer_norm(block_f, ln_gain, ln_bias, -1).astype(jnp.bfloat16)
        projected = jnp.dot(normed, w_qkv.reshape(D, 3 * width_heads), preferred_element_type=jnp.float32)
        projected = projected.reshape(TOK_DEV, 3, HEADS, HEAD_DIM)
        queries = rotate_pairs(projected[:, 0], row_index, col_index, is_patch).astype(jnp.bfloat16)
        keys_bf = rotate_pairs(projected[:, 1], row_index, col_index, is_patch).astype(jnp.bfloat16)
        values_bf = projected[:, 2].astype(jnp.bfloat16)
        scores = jnp.einsum('qhd,khd->hqk', queries.astype(jnp.float32), keys_bf.astype(jnp.float32)) * HEAD_DIM ** (-0.5)
        same = segment[:, None] == segment[None, :]
        scores = jnp.where(same[None], scores, -jnp.inf)
        top_score = lax.optimization_barrier(jnp.max(scores, axis=-1, keepdims=True))
        expo = jnp.exp(scores - top_score)
        probabilities = (expo / lax.optimization_barrier(jnp.sum(expo, axis=-1, keepdims=True))).astype(jnp.bfloat16)
        attended = jnp.einsum('hqk,khd->qhd', probabilities.astype(jnp.float32), values_bf.astype(jnp.float32))
        attended = attended.astype(jnp.bfloat16).reshape(TOK_DEV, width_heads)
        head_total = jnp.zeros((TOK_DEV, D), jnp.float32)
        for group in range(N_TENSOR):
            partial_out = jnp.dot(attended[:, group * group_cols:(group + 1) * group_cols], w_out[group * group_cols:(group + 1) * group_cols], preferred_element_type=jnp.float32)
            rounded = lax.optimization_barrier(partial_out.astype(jnp.bfloat16))
            head_total = head_total + rounded.astype(jnp.float32)
        residual = block_f + layer_scale * head_total
        groups = jnp.take(residual, sources, axis=0)
        merge_in = layer_norm(groups, merge_gain, merge_bias, (1, 2)).astype(jnp.bfloat16)
        merged_rows = jnp.dot(merge_in.reshape(MERGED_DEV, 4 * D), w_merge.reshape(4 * D, MERGE_OUT), preferred_element_type=jnp.float32).astype(jnp.bfloat16)
        position = route_slots(owner_dev, is_live, N_ROWS, slot_count)
        return (merged_rows, position)
    merged_rows, position = lax.map(per_device, (all_tokens, grid_sizes, all_owners))
    source_ids = jnp.arange(N_ROWS, dtype=jnp.int32)[:, None]
    limit = N_ROWS * slot_count
    target = jnp.where(position < limit, position // slot_count * limit + source_ids * slot_count + position % slot_count, N_ROWS * limit)
    output = jnp.zeros((N_ROWS * limit + 1, MERGE_OUT), jnp.bfloat16)
    output = output.at[target.reshape(-1)].set(merged_rows.reshape(-1, MERGE_OUT))
    return output[:-1]
```

```python
import functools
import math

import jax
import jax.numpy as jnp
from jax import lax
from jax.experimental import pallas as pl
from jax.experimental.pallas import tpu as pltpu
from jax.sharding import PartitionSpec as P

MESH = pl.DeviceIdType.MESH
F32 = jnp.float32
BF16 = jnp.bfloat16
HEAD_DIM = 128
PREFIX = 5


def image_layout(device_grid, tok_count, merged_count):
    heights = device_grid[:, 0]
    widths = device_grid[:, 1]
    image_total = device_grid.shape[0]
    lengths = PREFIX + heights * widths
    starts = jnp.cumsum(lengths, dtype=jnp.int32) - lengths
    positions = jnp.arange(tok_count, dtype=jnp.int32)
    inside = (
        (positions[:, None] >= starts[None, :]) & (positions[:, None] < (starts + lengths)[None, :])
    ).astype(jnp.int32)
    image_ids = jnp.arange(image_total, dtype=jnp.int32)
    occupied = jnp.sum(inside, axis=1, dtype=jnp.int32)
    segment = jnp.sum(inside * image_ids[None, :], axis=1, dtype=jnp.int32) + image_total * (
        1 - occupied
    )
    local_pos = positions - jnp.sum(inside * starts[None, :], axis=1, dtype=jnp.int32)
    width_here = jnp.maximum(jnp.sum(inside * widths[None, :], axis=1, dtype=jnp.int32), 1)
    is_patch = occupied * (local_pos >= PREFIX).astype(jnp.int32)
    flat_patch = jnp.maximum(local_pos - PREFIX, 0) * is_patch
    row_index = flat_patch // width_here
    col_index = flat_patch % width_here
    merged_counts = heights * widths // 4
    merged_starts = jnp.cumsum(merged_counts, dtype=jnp.int32) - merged_counts
    slot_ids = jnp.arange(merged_count, dtype=jnp.int32)
    within = (
        (slot_ids[:, None] >= merged_starts[None, :])
        & (slot_ids[:, None] < (merged_starts + merged_counts)[None, :])
    ).astype(jnp.int32)
    is_live = jnp.sum(within, axis=1, dtype=jnp.int32)
    slot_image = jnp.sum(within * image_ids[None, :], axis=1, dtype=jnp.int32)
    offset_in = slot_ids - jnp.sum(within * merged_starts[None, :], axis=1, dtype=jnp.int32)
    image_width = jnp.sum(within * widths[None, :], axis=1, dtype=jnp.int32)
    half_width = jnp.maximum(image_width // 2, 1)
    first_patch = jnp.sum(within * starts[None, :], axis=1, dtype=jnp.int32) + PREFIX
    merged_row = offset_in // half_width
    merged_col = offset_in % half_width
    picks = []
    for down in (0, 1):
        for across in (0, 1):
            picks.append(
                first_patch + (2 * merged_row + down) * image_width + 2 * merged_col + across
            )
    sources = jnp.stack(picks, axis=0) * is_live[None, :]
    return segment, row_index, col_index, is_patch, sources, is_live, slot_image


def outgoing_rows(owner_dev, is_live, rows_count, stride):
    hits = (owner_dev[:, None] == jnp.arange(rows_count, dtype=jnp.int32)[None, :]).astype(
        jnp.int32
    ) * is_live[:, None]
    before = jnp.cumsum(hits, axis=0, dtype=jnp.int32) - hits
    ranking = jnp.sum(before * hits, axis=1, dtype=jnp.int32)
    return jnp.where(is_live > 0, owner_dev * stride + ranking, -1)


def rotation_tables(row_index, col_index, is_patch):
    lane = jnp.arange(HEAD_DIM, dtype=jnp.int32)
    quarter = HEAD_DIM // 4
    freqs = 100.0 ** (-(lane % quarter).astype(F32) / quarter)
    coord = jnp.where(lane[None, :] < 2 * quarter, row_index[:, None], col_index[:, None])
    angle = (coord * is_patch[:, None]).astype(F32) * freqs[None, :]
    sign = jnp.where(lane % (2 * quarter) < quarter, -1.0, 1.0)
    return jnp.cos(angle), jnp.sin(angle) * sign[None, :]


class Gather:
    def __init__(self, src, buf, send, recv, place):
        self.src, self.buf, self.send, self.recv_sem = src, buf, send, recv
        self.y, self.x, self.t = place
        table = [
            ((0, 0), None, (1, 0)),
            ((0, 0), None, (-1, 0)),
            ((0, 0), None, (0, 1)),
            ((0, 0), None, (0, -1)),
            ((-1, 0), 0, (1, 0)),
            ((1, 0), 1, (-1, 0)),
            ((-1, 0), None, (0, 1)),
            ((-1, 0), None, (0, -1)),
            ((1, 0), None, (0, 1)),
            ((1, 0), None, (0, -1)),
            ((2, 0), None, (0, 1)),
            ((2, 0), None, (0, -1)),
        ]
        for first in (0, -1, 1, 2):
            table.append(((first, -1), 0, (0, 1)))
            table.append(((first, 1), 1, (0, -1)))
        self.table = table

    def slot(self, half, first, second):
        dx, dy = (first, second) if half == 0 else (second, first)
        return lax.rem(self.y + (dy % 4), 4) * 4 + lax.rem(self.x + (dx % 4), 4)

    def copy(self, half, i):
        (first, second), part, to = self.table[i]
        slot = self.slot(half, first, second)
        dst = self.buf.at[half, slot] if part is None else self.buf.at[half, slot, part]
        src = self.src.at[half] if self.src is not None and i < 4 else dst
        return pltpu.make_async_remote_copy(
            src_ref=src,
            dst_ref=dst,
            send_sem=self.send.at[half, i],
            recv_sem=self.recv_sem.at[half, i],
            device_id=(self.slot(half, *to), self.t),
            device_id_type=MESH,
        )

    def start(self, *which):
        for i in which:
            for half in (0, 1):
                self.copy(half, i).start()

    def recv(self, *which):
        for i in which:
            for half in (0, 1):
                self.copy(half, i).wait_recv()

    def r1(self):
        self.start(0, 1, 2, 3)

    def r2(self):
        self.recv(0, 1)
        self.start(4, 5, 6, 7, 8, 9)

    def r3(self):
        self.recv(4, 5)
        self.start(10, 11)

    def r4a(self):
        self.recv(2, 3)
        self.start(12, 13)

    def r4b(self):
        self.recv(6, 7, 8, 9)
        self.start(14, 15, 16, 17)

    def r4c(self):
        self.recv(10, 11)
        self.start(18, 19)

    def finish(self):
        self.recv(12, 13, 14, 15, 16, 17, 18, 19)

    def drain(self):
        for i in range(20):
            for half in (0, 1):
                self.copy(half, i).wait_send()


def dot(a, b):
    return jnp.dot(a, b, preferred_element_type=F32)


def kernel(
    tokens,
    wq,
    wo,
    wm,
    ln_gain,
    ln_bias,
    scale,
    merge_gain,
    merge_bias,
    cos_ref,
    sin_ref,
    segk_ref,
    segq_ref,
    src_ref,
    pos_ref,
    out,
    bufq,
    bufo,
    bufm,
    normed,
    acc,
    qb,
    kb,
    vb,
    att,
    tok,
    tokp,
    fromsib,
    oppa,
    oppb,
    zprev,
    znext,
    stats,
    mpart,
    msib,
    mz,
    obuf,
    sq,
    rq,
    so,
    ro,
    sm,
    rm,
    local,
    sperm,
    rperm,
    ssib,
    rsib,
    sopp,
    ropp,
    sz,
    rz,
    sstat,
    rstat,
    smsib,
    rmsib,
    smz,
    rmz,
    sout,
    rout,
):
    r = lax.axis_index("rows")
    t = lax.axis_index("tensor")
    y, x = lax.div(r, 4), lax.rem(r, 4)
    z, c = lax.div(t, 2), lax.rem(t, 2)
    place = (y, x, t)
    tiles = 4
    rows_tile = 256

    def zdev(offset, core=None):
        return lax.rem(z + offset % 4, 4) * 2 + (c if core is None else core)

    sibling = z * 2 + (1 - c)
    perm_to = ((1 - lax.rem(r, 2)) * 8 + t, lax.div(r, 2))
    perm_from = (2 * t + 1 - lax.div(r, 8), lax.rem(r, 8))

    barrier = pltpu.get_barrier_semaphore()
    for step in range(1, 16):
        pl.semaphore_signal(
            barrier, inc=1, device_id=(lax.rem(r + step, 16), t), device_id_type=MESH
        )
    for step in range(1, 8):
        pl.semaphore_signal(
            barrier, inc=1, device_id=(r, lax.rem(t + step, 8)), device_id_type=MESH
        )
    pl.semaphore_signal(barrier, inc=1, device_id=perm_from, device_id_type=MESH)
    pl.semaphore_wait(barrier, 23)

    gq = Gather(wq, bufq, sq, rq, place)
    go = Gather(wo, bufo, so, ro, place)
    gm = Gather(None, bufm, sm, rm, place)

    gq.r1()

    def perm_copy(half):
        return pltpu.make_async_remote_copy(
            src_ref=wm.at[half],
            dst_ref=bufm.at[half, perm_to[0]],
            send_sem=sperm.at[half],
            recv_sem=rperm.at[half],
            device_id=perm_to,
            device_id_type=MESH,
        )

    def perm_wait(half):
        pltpu.make_async_remote_copy(
            src_ref=wm.at[half],
            dst_ref=bufm.at[half, r],
            send_sem=sperm.at[half],
            recv_sem=rperm.at[half],
            device_id=perm_to,
            device_id_type=MESH,
        ).wait_recv()

    chunk = 256

    def tok_copy(i):
        rows = pl.ds(i * chunk, chunk)
        return pltpu.make_async_copy(tokens.at[rows], normed.at[rows], local.at[i])

    for i in range(4):
        tok_copy(i).start()
    own_q = [pltpu.make_async_copy(wq.at[h], bufq.at[h, r], local.at[4 + h]) for h in (0, 1)]
    own_o = [pltpu.make_async_copy(wo.at[h], bufo.at[h, r], local.at[6 + h]) for h in (0, 1)]
    columns = pl.ds(pl.multiple_of(t * 512, 512), 512)
    own_tok = pltpu.make_async_copy(tokens.at[:, columns], tok, local.at[8])
    for copy in own_q + own_o + [own_tok]:
        copy.start()
    for half in (0, 1):
        perm_copy(half).start()

    def norm_chunk(i):
        tok_copy(i).wait()
        step = 16

        def body(j, carry):
            at = pl.ds(pl.multiple_of(i * chunk + j * step, step), step)
            v = normed[at, :].astype(F32)
            mean = jnp.mean(v, axis=-1, keepdims=True)
            v = v - mean
            var = jnp.mean(v * v, axis=-1, keepdims=True)
            v = v * lax.rsqrt(var + 1e-6) * ln_gain[...] + ln_bias[...]
            normed[at, :] = v.astype(BF16)
            return carry

        lax.fori_loop(0, chunk // step, body, 0)

    for i in range(4):
        norm_chunk(i)

    def project(slots, first=False):
        for half in (0, 1):
            where = [gq.slot(half, *s) for s in slots]

            def body(i, carry, half=half, where=where):
                at = pl.ds(pl.multiple_of(i * rows_tile, rows_tile), rows_tile)
                total = None
                for w in where:
                    cols = pl.ds(pl.multiple_of(w * 256, 256), 256)
                    term = dot(normed[at, cols], bufq[half, w].reshape(256, 768))
                    total = term if total is None else total + term
                if first:
                    acc[half, at, :] = total
                else:
                    acc[half, at, :] += total
                return carry

            lax.fori_loop(0, tiles, body, 0)

    for copy in own_q:
        copy.wait()
    gq.r2()
    gq.r4a()
    project([(0, 0), (-1, 0), (1, 0)], first=True)
    project([(0, -1), (0, 1)])
    gq.r3()
    project([(2, 0)])
    for half in (0, 1):
        perm_wait(half)
    for copy in own_o + [own_tok]:
        copy.wait()
    go.r1()
    gq.r4b()
    project([(-1, -1), (-1, 1), (1, -1), (1, 1)])
    gq.r4c()
    go.r2()
    go.r4a()
    project([(2, -1), (2, 1)])
    gq.recv(12, 13, 14, 15)
    project([(0, 2), (-1, 2)])
    go.r3()
    gm.r1()
    gq.recv(16, 17, 18, 19)
    project([(1, 2), (2, 2)])
    go.r4b()
    gm.r2()
    gm.r4a()

    lane = lax.broadcasted_iota(jnp.int32, (rows_tile, HEAD_DIM), 1)
    low = lax.rem(lane, 64) < 32

    def rotate(i, carry):
        at = pl.ds(pl.multiple_of(i * rows_tile, rows_tile), rows_tile)
        cosine, sine = cos_ref[at, :], sin_ref[at, :]
        for head in range(4):
            half, inner = divmod(head, 2)
            for dst, base in ((qb, 0), (kb, 256)):
                v = acc[half, at, base + inner * 128 : base + inner * 128 + 128]
                partner = jnp.where(low, pltpu.roll(v, 96, 1), pltpu.roll(v, 32, 1))
                dst[at, head * 128 : head * 128 + 128] = (v * cosine + partner * sine).astype(BF16)
            vb[at, head * 128 : head * 128 + 128] = acc[
                half, at, 512 + inner * 128 : 512 + inner * 128 + 128
            ].astype(BF16)
        return carry

    lax.fori_loop(0, tiles, rotate, 0)

    factor = HEAD_DIM ** (-0.5) / math.log(2.0)

    def attend(k):
        at = slice(k * rows_tile, (k + 1) * rows_tile)
        pick = (
            lax.broadcasted_iota(jnp.int32, (rows_tile, 1024), 1) == src_ref[at, :]
        ).astype(BF16)
        att[at, :] = dot(pick, qb[...]).astype(BF16)
        tokp[at, :] = dot(pick, tok[...]).astype(BF16)

        def body(head, carry):
            cols = pl.ds(pl.multiple_of(head * 128, 128), 128)
            s = lax.dot_general(
                att[at, cols], kb[:, cols], (((1,), (1,)), ((), ())), preferred_element_type=F32
            )
            s = jnp.where(segq_ref[at, :] == segk_ref[...], s, -jnp.inf)
            top = jnp.max(s, axis=-1, keepdims=True)
            e = jnp.exp2((s - top) * factor)
            total = jnp.sum(e, axis=-1, keepdims=True)
            o = dot(e.astype(BF16), vb[:, cols])
            att[at, cols] = (o / total).astype(BF16)
            return carry

        lax.fori_loop(0, 4, body, 0)

    def out_project(k, core):
        at = slice(k * rows_tile, (k + 1) * rows_tile)

        def body(i, carry):
            slot = lax.div(i, 2) * 4 + core * 2 + lax.rem(i, 2)
            total = dot(att[at, 0:256], bufo[0, slot].reshape(256, 256)) + dot(
                att[at, 256:512], bufo[1, slot].reshape(256, 256)
            )
            normed[at, pl.ds(pl.multiple_of(slot * 256, 256), 256)] = total.astype(BF16)
            return carry

        lax.fori_loop(0, 8, body, 0)

    def chunk_of(k, tensor, lo=0, hi=256):
        return normed.at[
            pl.ds(k * rows_tile + lo, hi - lo), pl.ds(pl.multiple_of(tensor * 512, 512), 512)
        ]

    def sib_copy(k, zz):
        return pltpu.make_async_remote_copy(
            src_ref=chunk_of(k, zz * 2 + (1 - c)),
            dst_ref=fromsib.at[k, zz],
            send_sem=ssib.at[k, zz],
            recv_sem=rsib.at[k, zz],
            device_id=(r, sibling),
            device_id_type=MESH,
        )

    def opp_copy(k, which):
        lo = 128 * which
        return pltpu.make_async_remote_copy(
            src_ref=chunk_of(k, zdev(2), lo, lo + 128),
            dst_ref=(oppa, oppb)[which].at[k],
            send_sem=sopp.at[k, which],
            recv_sem=ropp.at[k, which],
            device_id=(r, zdev(1 if which == 0 else -1)),
            device_id_type=MESH,
        )

    def z_copy(k, which):
        to = zdev(1 if which == 0 else -1)
        return pltpu.make_async_remote_copy(
            src_ref=chunk_of(k, to),
            dst_ref=(zprev, znext)[which].at[k],
            send_sem=sz.at[k, which],
            recv_sem=rz.at[k, which],
            device_id=(r, to),
            device_id_type=MESH,
        )

    def stage1(k):
        out_project(k, 1 - c)
        for zz in range(4):
            sib_copy(k, zz).start()
        out_project(k, c)

    def stage2(k):
        for zz in range(4):
            sib_copy(k, zz).wait_recv()

        def body(zz, carry):
            ref = chunk_of(k, zz * 2 + c)
            ref[...] = (ref[...].astype(F32) + fromsib[k, zz].astype(F32)).astype(BF16)
            return carry

        lax.fori_loop(0, 4, body, 0)
        for which in (0, 1):
            opp_copy(k, which).start()

    def stage3(k):
        for which, lo in ((0, 0), (1, 128)):
            opp_copy(k, which).wait_recv()
            ref = chunk_of(k, zdev(1 if which == 0 else -1), lo, lo + 128)
            ref[...] = (ref[...].astype(F32) + (oppa, oppb)[which][k].astype(F32)).astype(BF16)
            z_copy(k, which).start()

    sums = []

    def stage4(k):
        at = slice(k * rows_tile, (k + 1) * rows_tile)
        for which in (0, 1):
            z_copy(k, which).wait_recv()
        total = (
            chunk_of(k, t)[...].astype(F32) + zprev[k].astype(F32) + znext[k].astype(F32)
        )
        res = tokp[at, :].astype(F32) + scale[:, columns] * total
        acc[0, at, 0:512] = res
        sums.append(jnp.sum(res, axis=-1, keepdims=True))

    attend(0)
    go.r4c()
    gm.r3()
    attend(1)
    go.finish()
    gm.r4b()
    stage1(0)
    attend(2)
    stage2(0)
    stage1(1)
    attend(3)
    stage3(0)
    stage2(1)
    stage1(2)
    gm.r4c()
    stage3(1)
    stage2(2)
    stage1(3)
    stage3(2)
    stage2(3)
    stage4(0)
    stage4(1)
    stage3(3)
    stage4(2)
    stage4(3)

    mean_l = (sums[0] + sums[1] + sums[2] + sums[3]) * (1.0 / 2048)
    m2 = None
    for k in range(4):
        d = acc[0, k * 256 : (k + 1) * 256, 0:512] - mean_l
        term = jnp.sum(d * d, axis=-1, keepdims=True)
        m2 = term if m2 is None else m2 + term
    packed = jnp.where(lane == 0, mean_l, m2)
    stats[0] = packed.T[0:8, :]

    def stat_copy(step):
        return pltpu.make_async_remote_copy(
            src_ref=stats.at[0],
            dst_ref=stats.at[step],
            send_sem=sstat.at[step],
            recv_sem=rstat.at[step],
            device_id=(r, lax.rem(t + step, 8)),
            device_id_type=MESH,
        )

    for step in range(1, 8):
        stat_copy(step).start()
    gm.finish()
    for step in range(1, 8):
        stat_copy(step).wait_recv()
    means = [stats[i][0:1, :] for i in range(8)]
    m2s = [stats[i][1:2, :] for i in range(8)]
    mean = functools.reduce(lambda a, b: a + b, means) * 0.125
    total2 = functools.reduce(lambda a, b: a + b, m2s)
    for m in means:
        total2 = total2 + 2048.0 * (m - mean) * (m - mean)
    rs = lax.rsqrt(total2 * (1.0 / 16384) + 1e-6)
    row = lax.broadcasted_iota(jnp.int32, (128, 256), 0)
    back = jnp.where(row == 0, mean, rs).T
    mean_c, rs_c = back[:, 0:1], back[:, 1:2]
    for k in range(4):
        at = slice(k * rows_tile, (k + 1) * rows_tile)
        v = (acc[0, at, 0:512] - mean_c) * rs_c
        v = v * merge_gain[k : k + 1, columns] + merge_bias[k : k + 1, columns]
        att[at, :] = v.astype(BF16)

    def merge_project(core):
        def body(zz, carry):
            total = None
            for k in range(4):
                for b in (0, 1):
                    slot = (1 - b) * 8 + zz * 2 + core
                    term = dot(
                        att[k * 256 : (k + 1) * 256, b * 256 : b * 256 + 256],
                        bufm[k // 2, slot, k % 2],
                    )
                    total = term if total is None else total + term
            mpart[core, zz] = total.astype(BF16)
            return carry

        lax.fori_loop(0, 4, body, 0)

    def msib_copy():
        return pltpu.make_async_remote_copy(
            src_ref=mpart.at[1 - c],
            dst_ref=msib,
            send_sem=smsib,
            recv_sem=rmsib,
            device_id=(r, sibling),
            device_id_type=MESH,
        )

    merge_project(1 - c)
    msib_copy().start()
    merge_project(c)
    msib_copy().wait_recv()

    def mz_copy(step):
        zz = lax.rem(z + step, 4)
        return pltpu.make_async_remote_copy(
            src_ref=mpart.at[c, zz],
            dst_ref=mz.at[step - 1],
            send_sem=smz.at[step - 1],
            recv_sem=rmz.at[step - 1],
            device_id=(r, zz * 2 + c),
            device_id_type=MESH,
        )

    for step in (2, 1, 3):
        zz = lax.rem(z + step, 4)
        mpart[c, zz] = (mpart[c, zz].astype(F32) + msib[zz].astype(F32)).astype(BF16)
        mz_copy(step).start()
    merged = mpart[c, z].astype(F32) + msib[z].astype(F32)
    for step in (1, 3, 2):
        mz_copy(step).wait_recv()
        merged = merged + mz[step - 1].astype(F32)
    merged = merged.astype(BF16)

    place_row = (lax.broadcasted_iota(jnp.int32, (512, 256), 0) == pos_ref[...]).astype(BF16)
    obuf[...] = dot(place_row, merged).astype(BF16).reshape(16, 32, 256)

    def out_copy(step):
        to = lax.rem(r + step, 16)
        return pltpu.make_async_remote_copy(
            src_ref=obuf.at[to],
            dst_ref=out.at[r],
            send_sem=sout.at[step],
            recv_sem=rout.at[step],
            device_id=(to, t),
            device_id_type=MESH,
        )

    def out_wait(step):
        come = lax.rem(r + 16 - step, 16)
        pltpu.make_async_remote_copy(
            src_ref=obuf.at[come],
            dst_ref=out.at[come],
            send_sem=sout.at[step],
            recv_sem=rout.at[step],
            device_id=(come, t),
            device_id_type=MESH,
        ).wait_recv()

    own_out = pltpu.make_async_copy(obuf.at[r], out.at[r], local.at[9])
    for step in range(1, 16):
        out_copy(step).start()
    own_out.start()

    for half in (0, 1):
        perm_copy(half).wait_send()
    for g in (gq, go, gm):
        g.drain()
    for k in range(4):
        for zz in range(4):
            sib_copy(k, zz).wait_send()
        for which in (0, 1):
            opp_copy(k, which).wait_send()
            z_copy(k, which).wait_send()
    for step in range(1, 8):
        stat_copy(step).wait_send()
    msib_copy().wait_send()
    for step in (1, 2, 3):
        mz_copy(step).wait_send()
    own_out.wait()
    for step in range(1, 16):
        out_wait(step)
        out_copy(step).wait_send()


def per_device(
    tokens,
    grid_sizes,
    owners,
    ln_gain,
    ln_bias,
    w_qkv,
    w_out,
    layer_scale,
    merge_gain,
    merge_bias,
    w_merge,
):
    rows_index = lax.axis_index("rows")
    device_grid = lax.dynamic_index_in_dim(grid_sizes, rows_index, 0, keepdims=False)
    segment, row_index, col_index, is_patch, sources, is_live, slot_image = image_layout(
        device_grid, 1024, 256
    )
    cosine, sine = rotation_tables(row_index, col_index, is_patch)
    owner_dev = lax.dynamic_slice_in_dim(owners[:, 0], rows_index * 256, 256)
    position = outgoing_rows(owner_dev, is_live, 16, 32)
    wq = w_qkv.reshape(2, 128, 3, 2, 256).transpose(3, 0, 1, 2, 4).reshape(2, 2, 128, 768)
    wo = w_out.reshape(2, 2, 128, 256)
    wm = w_merge.reshape(2, 2, 256, 256)

    any_space = pl.BlockSpec(memory_space=pl.ANY)
    vmem = pl.BlockSpec(memory_space=pltpu.VMEM)
    dma = pltpu.SemaphoreType.DMA
    out = pl.pallas_call(
        kernel,
        out_shape=jax.ShapeDtypeStruct((16, 32, 256), BF16),
        in_specs=[any_space] * 4 + [vmem] * 11,
        out_specs=any_space,
        scratch_shapes=[
            pltpu.VMEM((2, 16, 2, 128, 768), BF16),
            pltpu.VMEM((2, 16, 2, 128, 256), BF16),
            pltpu.VMEM((2, 16, 2, 256, 256), BF16),
            pltpu.VMEM((1024, 4096), BF16),
            pltpu.VMEM((2, 1024, 768), F32),
            pltpu.VMEM((1024, 512), BF16),
            pltpu.VMEM((1024, 512), BF16),
            pltpu.VMEM((1024, 512), BF16),
            pltpu.VMEM((1024, 512), BF16),
            pltpu.VMEM((1024, 512), BF16),
            pltpu.VMEM((1024, 512), BF16),
            pltpu.VMEM((4, 4, 256, 512), BF16),
            pltpu.VMEM((4, 128, 512), BF16),
            pltpu.VMEM((4, 128, 512), BF16),
            pltpu.VMEM((4, 256, 512), BF16),
            pltpu.VMEM((4, 256, 512), BF16),
            pltpu.VMEM((8, 8, 256), F32),
            pltpu.VMEM((2, 4, 256, 256), BF16),
            pltpu.VMEM((4, 256, 256), BF16),
            pltpu.VMEM((3, 256, 256), BF16),
            pltpu.VMEM((16, 32, 256), BF16),
            dma((2, 20)),
            dma((2, 20)),
            dma((2, 20)),
            dma((2, 20)),
            dma((2, 20)),
            dma((2, 20)),
            dma((10,)),
            dma((2,)),
            dma((2,)),
            dma((4, 4)),
            dma((4, 4)),
            dma((4, 2)),
            dma((4, 2)),
            dma((4, 2)),
            dma((4, 2)),
            dma((8,)),
            dma((8,)),
            dma,
            dma,
            dma((3,)),
            dma((3,)),
            dma((16,)),
            dma((16,)),
        ],
        compiler_params=pltpu.CompilerParams(
            collective_id=0, has_side_effects=True, vmem_limit_bytes=63 * 2**20
        ),
    )(
        tokens,
        wq,
        wo,
        wm,
        ln_gain[None],
        ln_bias[None],
        layer_scale[None],
        merge_gain,
        merge_bias,
        cosine,
        sine,
        segment[None],
        jnp.tile(slot_image, 4)[:, None],
        sources.reshape(1024, 1),
        position[None],
    )
    return out[:, :24].reshape(384, 256)


def solution(mesh):
    return jax.shard_map(
        per_device,
        mesh=mesh,
        in_specs=(
            P("rows", None),
            P(),
            P(),
            P(),
            P(),
            P("rows", None, "tensor"),
            P("tensor", "rows"),
            P(),
            P(),
            P(),
            P(None, "rows", "tensor"),
        ),
        out_specs=P("rows", "tensor"),
        check_vma=False,
    )
```

```python
import functools
import math

import jax
import jax.numpy as jnp
from jax import lax
from jax.experimental import pallas as pl
from jax.experimental.pallas import tpu as pltpu
from jax.sharding import PartitionSpec as P

MESH = pl.DeviceIdType.MESH
F32 = jnp.float32
BF16 = jnp.bfloat16
HEAD_DIM = 128
PREFIX = 5


class Gather:
    def __init__(self, src, buf, send, recv, place):
        self.src, self.buf, self.send, self.recv_sem = src, buf, send, recv
        self.y, self.x, self.t = place
        table = [
            ((0, 0), None, (1, 0)),
            ((0, 0), None, (-1, 0)),
            ((0, 0), None, (0, 1)),
            ((0, 0), None, (0, -1)),
            ((-1, 0), 0, (1, 0)),
            ((1, 0), 1, (-1, 0)),
            ((-1, 0), None, (0, 1)),
            ((-1, 0), None, (0, -1)),
            ((1, 0), None, (0, 1)),
            ((1, 0), None, (0, -1)),
            ((2, 0), None, (0, 1)),
            ((2, 0), None, (0, -1)),
        ]
        for first in (0, -1, 1, 2):
            table.append(((first, -1), 0, (0, 1)))
            table.append(((first, 1), 1, (0, -1)))
        self.table = table

    def slot(self, half, first, second):
        dx, dy = (first, second) if half == 0 else (second, first)
        return lax.rem(self.y + (dy % 4), 4) * 4 + lax.rem(self.x + (dx % 4), 4)

    def copy(self, half, i):
        (first, second), part, to = self.table[i]
        slot = self.slot(half, first, second)
        dst = self.buf.at[half, slot] if part is None else self.buf.at[half, slot, part]
        src = self.src.at[half] if self.src is not None and i < 4 else dst
        return pltpu.make_async_remote_copy(
            src_ref=src,
            dst_ref=dst,
            send_sem=self.send.at[half, i],
            recv_sem=self.recv_sem.at[half, i],
            device_id=(self.slot(half, *to), self.t),
            device_id_type=MESH,
        )

    def start(self, *which):
        for i in which:
            for half in (0, 1):
                self.copy(half, i).start()

    def recv(self, *which):
        for i in which:
            for half in (0, 1):
                self.copy(half, i).wait_recv()

    def r1(self):
        self.start(0, 1, 2, 3)

    def r2(self):
        self.recv(0, 1)
        self.start(4, 5, 6, 7, 8, 9)

    def r3(self):
        self.recv(4, 5)
        self.start(10, 11)

    def r4a(self):
        self.recv(2, 3)
        self.start(12, 13)

    def r4b(self):
        self.recv(6, 7, 8, 9)
        self.start(14, 15, 16, 17)

    def r4c(self):
        self.recv(10, 11)
        self.start(18, 19)

    def finish(self):
        self.recv(12, 13, 14, 15, 16, 17, 18, 19)

    def drain(self):
        for i in range(20):
            for half in (0, 1):
                self.copy(half, i).wait_send()


def dot(a, b):
    return jnp.dot(a, b, preferred_element_type=F32)


def kernel(
    tokens,
    wq,
    wo,
    wm,
    ln_gain,
    ln_bias,
    scale,
    merge_gain,
    merge_bias,
    freq_ref,
    grid_ref,
    own_ref,
    out,
    bufq,
    bufo,
    bufm,
    normed,
    acc,
    qb,
    kb,
    vb,
    att,
    tok,
    tokp,
    cos_ref,
    sin_ref,
    src_ref,
    segq_ref,
    pos_ref,
    fromsib,
    oppa,
    oppb,
    zprev,
    znext,
    stats,
    mpart,
    msib,
    mz,
    obuf,
    sq,
    rq,
    so,
    ro,
    sm,
    rm,
    local,
    sperm,
    rperm,
    ssib,
    rsib,
    sopp,
    ropp,
    sz,
    rz,
    sstat,
    rstat,
    smsib,
    rmsib,
    smz,
    rmz,
    sout,
    rout,
):
    r = lax.axis_index("rows")
    t = lax.axis_index("tensor")
    y, x = lax.div(r, 4), lax.rem(r, 4)
    z, c = lax.div(t, 2), lax.rem(t, 2)
    place = (y, x, t)
    tiles = 4
    rows_tile = 256

    def zdev(offset, core=None):
        return lax.rem(z + offset % 4, 4) * 2 + (c if core is None else core)

    sibling = z * 2 + (1 - c)
    moved = lax.rem(x, 2)
    stays = c != lax.div(x, 2)
    to_x = jnp.where(stays, x, lax.rem(x + 2 * moved + 3, 4))
    perm_to = (lax.rem(y + z, 4) * 4 + to_x, y * 2 + lax.div(x, 2))
    from_z = lax.rem(y + 4 - z, 4)
    same = lax.div(x, 2) == c
    from_x = jnp.where(same, x, 2 * c + 1 - lax.rem(x, 2))
    perm_from = (z * 4 + from_x, from_z * 2 + jnp.where(same, 1 - c, c))

    def dealt_slot(b, zz, core):
        stay_x = 2 * c + b
        move_x = lax.rem(2 * c + b + 2 * b + 3, 4)
        return lax.rem(z + zz, 4) * 4 + jnp.where(core == c, move_x, stay_x)

    barrier = pltpu.get_barrier_semaphore()
    for step in range(1, 16):
        pl.semaphore_signal(
            barrier, inc=1, device_id=(lax.rem(r + step, 16), t), device_id_type=MESH
        )
    for step in range(1, 8):
        pl.semaphore_signal(
            barrier, inc=1, device_id=(r, lax.rem(t + step, 8)), device_id_type=MESH
        )
    pl.semaphore_signal(barrier, inc=1, device_id=perm_from, device_id_type=MESH)
    pl.semaphore_wait(barrier, 23)

    gq = Gather(wq, bufq, sq, rq, place)
    go = Gather(wo, bufo, so, ro, place)
    gm = Gather(None, bufm, sm, rm, place)

    gq.r1()

    def perm_copy(half):
        return pltpu.make_async_remote_copy(
            src_ref=wm.at[half],
            dst_ref=bufm.at[half, perm_to[0]],
            send_sem=sperm.at[half],
            recv_sem=rperm.at[half],
            device_id=perm_to,
            device_id_type=MESH,
        )

    def perm_wait(half):
        pltpu.make_async_remote_copy(
            src_ref=wm.at[half],
            dst_ref=bufm.at[half, r],
            send_sem=sperm.at[half],
            recv_sem=rperm.at[half],
            device_id=perm_to,
            device_id_type=MESH,
        ).wait_recv()

    chunk = 256

    def tok_copy(i):
        rows = pl.ds(i * chunk, chunk)
        return pltpu.make_async_copy(tokens.at[rows], normed.at[rows], local.at[i])

    for i in range(4):
        tok_copy(i).start()
    own_q = [pltpu.make_async_copy(wq.at[h], bufq.at[h, r], local.at[4 + h]) for h in (0, 1)]
    own_o = [pltpu.make_async_copy(wo.at[h], bufo.at[h, r], local.at[6 + h]) for h in (0, 1)]
    columns = pl.ds(pl.multiple_of(t * 512, 512), 512)
    own_tok = pltpu.make_async_copy(tokens.at[:, columns], tok, local.at[8])
    for copy in own_q + own_o + [own_tok]:
        copy.start()
    for half in (0, 1):
        perm_copy(half).start()

    def norm_chunk(i):
        tok_copy(i).wait()
        step = 16

        def body(j, carry):
            at = pl.ds(pl.multiple_of(i * chunk + j * step, step), step)
            v = normed[at, :].astype(F32)
            mean = jnp.mean(v, axis=-1, keepdims=True)
            v = v - mean
            var = jnp.mean(v * v, axis=-1, keepdims=True)
            v = v * lax.rsqrt(var + 1e-6) * ln_gain[...] + ln_bias[...]
            normed[at, :] = v.astype(BF16)
            return carry

        lax.fori_loop(0, chunk // step, body, 0)

    heights = [grid_ref[r, i, 0] for i in range(4)]
    widths = [grid_ref[r, i, 1] for i in range(4)]
    starts, merged_starts = [jnp.int32(0)], [jnp.int32(0)]
    for h, w in zip(heights, widths):
        starts.append(starts[-1] + PREFIX + h * w)
        merged_starts.append(merged_starts[-1] + lax.div(h * w, 4))
    lane = lax.broadcasted_iota(jnp.int32, (rows_tile, HEAD_DIM), 1)
    low = lax.rem(lane, 64) < 32

    def choose(at, edges, values):
        chosen = jnp.full(at.shape, values[0], jnp.int32)
        for edge, value in zip(edges[1:4], values[1:4]):
            chosen = jnp.where(at >= edge, value, chosen)
        return chosen

    def tables(i, carry):
        at = pl.ds(pl.multiple_of(i * rows_tile, rows_tile), rows_tile)
        pos = lax.broadcasted_iota(jnp.int32, (rows_tile, HEAD_DIM), 0) + i * rows_tile
        local_pos = pos - choose(pos, starts, starts) - PREFIX
        patch = (local_pos >= 0) & (pos < starts[4])
        flat = jnp.where(patch, local_pos, 0).astype(F32)
        width = choose(pos, starts, widths).astype(F32)
        row = jnp.floor((flat + 0.5) / width)
        angle = jnp.where(lane < 64, row, flat - row * width) * freq_ref[...]
        cos_ref[at, :] = jnp.cos(angle)
        sine = jnp.sin(angle)
        sin_ref[at, :] = jnp.where(low, -sine, sine)
        return carry

    def slots_layout():
        m = lax.broadcasted_iota(jnp.int32, (rows_tile, HEAD_DIM), 0)
        live = m < merged_starts[4]
        width = choose(m, merged_starts, widths).astype(F32)
        first = choose(m, merged_starts, starts).astype(F32) + PREFIX
        offset = (m - choose(m, merged_starts, merged_starts)).astype(F32)
        row = jnp.floor((offset + 0.5) / (0.5 * width))
        corner = first + (2.0 * row) * width + 2.0 * (offset - row * (0.5 * width))
        for k in range(4):
            source = corner + width * float(k // 2) + float(k % 2)
            src_ref[k * rows_tile : (k + 1) * rows_tile, :] = jnp.where(live, source, 0.0).astype(
                jnp.int32
            )
        segq_ref[...] = jnp.where(live, choose(m, merged_starts, [0, 1, 2, 3]), 0)

        own_row = own_ref[pl.ds(r, 1), :]
        own_col = jnp.broadcast_to(own_row.astype(F32), (HEAD_DIM, 256)).T[:, 0:1]
        before = lax.broadcasted_iota(jnp.int32, (256, 256), 0) < lax.broadcasted_iota(
            jnp.int32, (256, 256), 1
        )
        hit = before & (own_col == own_row.astype(F32))
        rank = jnp.sum(jnp.where(hit, 1.0, 0.0), axis=0, keepdims=True).astype(jnp.int32)
        live_row = lax.broadcasted_iota(jnp.int32, (1, 256), 1) < merged_starts[4]
        pos_ref[...] = jnp.where(live_row, own_row * 32 + rank, -1)

    key_pos = lax.broadcasted_iota(jnp.int32, (1, 1024), 1)
    segk = jnp.zeros((1, 1024), jnp.int32)
    for edge in starts[1:]:
        segk = segk + (key_pos >= edge).astype(jnp.int32)

    def project(slots, first=False):
        for half in (0, 1):
            where = [gq.slot(half, *s) for s in slots]

            def body(i, carry, half=half, where=where):
                out_cols = pl.ds(pl.multiple_of(i * 256, 256), 256)
                total = None
                for w in where:
                    cols = pl.ds(pl.multiple_of(w * 256, 256), 256)
                    term = dot(normed[:, cols], bufq[half, w, :, :, out_cols].reshape(256, 256))
                    total = term if total is None else total + term
                if first:
                    acc[half, :, out_cols] = total
                else:
                    acc[half, :, out_cols] += total
                return carry

            lax.fori_loop(0, 3, body, 0)

    for i in range(3):
        norm_chunk(i)
    for copy in own_q:
        copy.wait()
    gq.r2()
    norm_chunk(3)
    gq.r4a()
    project([(0, 0), (-1, 0), (1, 0)], first=True)
    project([(0, -1), (0, 1)])
    gq.r3()
    project([(2, 0)])
    lax.fori_loop(0, tiles, tables, 0)
    slots_layout()
    for copy in own_o + [own_tok]:
        copy.wait()
    gq.r4b()
    go.r1()
    project([(-1, -1), (-1, 1), (1, -1), (1, 1)])
    gq.r4c()
    project([(2, -1), (2, 1)])
    gq.recv(12, 13, 14, 15)
    project([(0, 2), (-1, 2)])
    go.r2()
    go.r4a()
    gq.recv(16, 17, 18, 19)
    project([(1, 2), (2, 2)])
    go.r3()

    def rotate(i, carry):
        at = pl.ds(pl.multiple_of(i * rows_tile, rows_tile), rows_tile)
        cosine, sine = cos_ref[at, :], sin_ref[at, :]
        for head in range(4):
            half, inner = divmod(head, 2)
            for dst, base in ((qb, 0), (kb, 256)):
                v = acc[half, at, base + inner * 128 : base + inner * 128 + 128]
                partner = jnp.where(low, pltpu.roll(v, 96, 1), pltpu.roll(v, 32, 1))
                dst[at, head * 128 : head * 128 + 128] = (v * cosine + partner * sine).astype(BF16)
            vb[at, head * 128 : head * 128 + 128] = acc[
                half, at, 512 + inner * 128 : 512 + inner * 128 + 128
            ].astype(BF16)
        return carry

    lax.fori_loop(0, tiles, rotate, 0)

    factor = HEAD_DIM ** (-0.5) / math.log(2.0)

    def attend(k):
        at = slice(k * rows_tile, (k + 1) * rows_tile)
        pick = (
            lax.broadcasted_iota(jnp.int32, (rows_tile, 1024), 1) == src_ref[at, 0:1]
        ).astype(BF16)
        att[at, :] = dot(pick, qb[...]).astype(BF16)
        tokp[at, :] = dot(pick, tok[...]).astype(BF16)

        def body(head, carry):
            cols = pl.ds(pl.multiple_of(head * 128, 128), 128)
            s = lax.dot_general(
                att[at, cols], kb[:, cols], (((1,), (1,)), ((), ())), preferred_element_type=F32
            )
            s = jnp.where(segq_ref[:, 0:1] == segk, s, -jnp.inf)
            top = jnp.max(s, axis=-1, keepdims=True)
            e = jnp.exp2((s - top) * factor)
            total = jnp.sum(e, axis=-1, keepdims=True)
            o = dot(e.astype(BF16), vb[:, cols])
            att[at, cols] = (o / total).astype(BF16)
            return carry

        lax.fori_loop(0, 4, body, 0)

    def out_project(to):
        def body(j, carry):
            slot = to * 2 + j
            total = dot(att[:, 0:256], bufo[0, slot].reshape(256, 256)) + dot(
                att[:, 256:512], bufo[1, slot].reshape(256, 256)
            )
            normed[:, pl.ds(pl.multiple_of(slot * 256, 256), 256)] = total.astype(BF16)
            return carry

        lax.fori_loop(0, 2, body, 0)

    def chunk_of(tensor, lo=0, rows=1024):
        return normed.at[pl.ds(lo, rows), pl.ds(pl.multiple_of(tensor * 512, 512), 512)]

    def sib_copy(dz):
        return pltpu.make_async_remote_copy(
            src_ref=chunk_of(zdev(dz, 1 - c)),
            dst_ref=fromsib.at[dz % 4],
            send_sem=ssib.at[dz % 4],
            recv_sem=rsib.at[dz % 4],
            device_id=(r, sibling),
            device_id_type=MESH,
        )

    def opp_copy(which):
        return pltpu.make_async_remote_copy(
            src_ref=chunk_of(zdev(2), 512 * which, 512),
            dst_ref=(oppa, oppb)[which],
            send_sem=sopp.at[which],
            recv_sem=ropp.at[which],
            device_id=(r, zdev(1 if which == 0 else -1)),
            device_id_type=MESH,
        )

    def z_copy(which, part):
        to = zdev(1 if which == 0 else -1)
        return pltpu.make_async_remote_copy(
            src_ref=chunk_of(to, 512 * part, 512),
            dst_ref=(zprev, znext)[which].at[pl.ds(512 * part, 512)],
            send_sem=sz.at[which, part],
            recv_sem=rz.at[which, part],
            device_id=(r, to),
            device_id_type=MESH,
        )

    def partial(dz):
        out_project(zdev(dz, 1 - c))
        sib_copy(dz).start()
        out_project(zdev(dz))

    def add_sibling(dz):
        sib_copy(dz).wait_recv()

        def body(i, carry):
            ref = chunk_of(zdev(dz), pl.multiple_of(i * 256, 256), 256)
            other = fromsib[dz % 4, pl.ds(pl.multiple_of(i * 256, 256), 256), :]
            ref[...] = (ref[...].astype(F32) + other.astype(F32)).astype(BF16)
            return carry

        lax.fori_loop(0, 4, body, 0)

    def pass_on(which):
        opp_copy(which).wait_recv()
        for i in (0, 1):
            ref = chunk_of(zdev(1 if which == 0 else -1), 512 * which + 256 * i, 256)
            other = (oppa, oppb)[which][256 * i : 256 * i + 256, :]
            ref[...] = (ref[...].astype(F32) + other.astype(F32)).astype(BF16)
        z_copy(which, which).start()

    sums = []

    def finish_rows(k):
        at = slice(k * rows_tile, (k + 1) * rows_tile)
        total = (
            chunk_of(t, k * rows_tile, rows_tile)[...].astype(F32)
            + fromsib[0, at, :].astype(F32)
            + zprev[at, :].astype(F32)
            + znext[at, :].astype(F32)
        )
        res = tokp[at, :].astype(F32) + scale[:, columns] * total
        acc[0, at, 0:512] = res
        sums.append(jnp.sum(res, axis=-1, keepdims=True))

    go.r4b()
    attend(0)
    go.r4c()
    for half in (0, 1):
        perm_wait(half)
    gm.r1()
    attend(1)
    attend(2)
    attend(3)
    go.finish()
    partial(2)
    gm.r2()
    partial(1)
    add_sibling(2)
    opp_copy(0).start()
    opp_copy(1).start()
    partial(-1)
    add_sibling(1)
    z_copy(0, 1).start()
    gm.r4a()
    add_sibling(-1)
    z_copy(1, 0).start()
    partial(0)
    gm.r3()
    pass_on(0)
    pass_on(1)
    gm.r4b()
    sib_copy(0).wait_recv()
    z_copy(0, 1).wait_recv()
    z_copy(1, 1).wait_recv()
    z_copy(0, 0).wait_recv()
    z_copy(1, 0).wait_recv()
    gm.r4c()
    for k in range(4):
        finish_rows(k)

    mean_l = (sums[0] + sums[1] + sums[2] + sums[3]) * (1.0 / 2048)
    m2 = None
    for k in range(4):
        d = acc[0, k * 256 : (k + 1) * 256, 0:512] - mean_l
        term = jnp.sum(d * d, axis=-1, keepdims=True)
        m2 = term if m2 is None else m2 + term
    packed = jnp.where(lane == 0, mean_l, m2)
    stats[0] = packed.T[0:8, :]

    def stat_copy(step):
        return pltpu.make_async_remote_copy(
            src_ref=stats.at[0],
            dst_ref=stats.at[step],
            send_sem=sstat.at[step],
            recv_sem=rstat.at[step],
            device_id=(r, lax.rem(t + step, 8)),
            device_id_type=MESH,
        )

    for step in range(1, 8):
        stat_copy(step).start()
    gm.finish()
    for step in range(1, 8):
        stat_copy(step).wait_recv()
    means = [stats[i][0:1, :] for i in range(8)]
    m2s = [stats[i][1:2, :] for i in range(8)]
    mean = functools.reduce(lambda a, b: a + b, means) * 0.125
    total2 = functools.reduce(lambda a, b: a + b, m2s)
    for m in means:
        total2 = total2 + 2048.0 * (m - mean) * (m - mean)
    rs = lax.rsqrt(total2 * (1.0 / 16384) + 1e-6)
    row = lax.broadcasted_iota(jnp.int32, (128, 256), 0)
    back = jnp.where(row == 0, mean, rs).T
    mean_c, rs_c = back[:, 0:1], back[:, 1:2]
    for k in range(4):
        at = slice(k * rows_tile, (k + 1) * rows_tile)
        v = (acc[0, at, 0:512] - mean_c) * rs_c
        v = v * merge_gain[k : k + 1, columns] + merge_bias[k : k + 1, columns]
        att[at, :] = v.astype(BF16)

    def merge_project(core):
        def body(zz, carry):
            total = None
            for k in range(4):
                for b in (0, 1):
                    slot = dealt_slot(b, zz, core)
                    term = dot(
                        att[k * 256 : (k + 1) * 256, b * 256 : b * 256 + 256],
                        bufm[k // 2, slot, k % 2],
                    )
                    total = term if total is None else total + term
            mpart[core, zz] = total.astype(BF16)
            return carry

        lax.fori_loop(0, 4, body, 0)

    def msib_copy():
        return pltpu.make_async_remote_copy(
            src_ref=mpart.at[1 - c],
            dst_ref=msib,
            send_sem=smsib,
            recv_sem=rmsib,
            device_id=(r, sibling),
            device_id_type=MESH,
        )

    merge_project(1 - c)
    msib_copy().start()
    merge_project(c)
    msib_copy().wait_recv()

    def mz_copy(step):
        zz = lax.rem(z + step, 4)
        return pltpu.make_async_remote_copy(
            src_ref=mpart.at[c, zz],
            dst_ref=mz.at[step - 1],
            send_sem=smz.at[step - 1],
            recv_sem=rmz.at[step - 1],
            device_id=(r, zz * 2 + c),
            device_id_type=MESH,
        )

    for step in (2, 1, 3):
        zz = lax.rem(z + step, 4)
        mpart[c, zz] = (mpart[c, zz].astype(F32) + msib[zz].astype(F32)).astype(BF16)
        mz_copy(step).start()
    merged = mpart[c, z].astype(F32) + msib[z].astype(F32)
    for step in (1, 3, 2):
        mz_copy(step).wait_recv()
        merged = merged + mz[step - 1].astype(F32)
    merged = merged.astype(BF16)

    place_row = (lax.broadcasted_iota(jnp.int32, (512, 256), 0) == pos_ref[...]).astype(BF16)
    obuf[...] = dot(place_row, merged).astype(BF16).reshape(16, 32, 256)

    def out_copy(step):
        to = lax.rem(r + step, 16)
        return pltpu.make_async_remote_copy(
            src_ref=obuf.at[to],
            dst_ref=out.at[r],
            send_sem=sout.at[step],
            recv_sem=rout.at[step],
            device_id=(to, t),
            device_id_type=MESH,
        )

    def out_wait(step):
        come = lax.rem(r + 16 - step, 16)
        pltpu.make_async_remote_copy(
            src_ref=obuf.at[come],
            dst_ref=out.at[come],
            send_sem=sout.at[step],
            recv_sem=rout.at[step],
            device_id=(come, t),
            device_id_type=MESH,
        ).wait_recv()

    own_out = pltpu.make_async_copy(obuf.at[r], out.at[r], local.at[9])
    for step in range(1, 16):
        out_copy(step).start()
    own_out.start()

    for half in (0, 1):
        perm_copy(half).wait_send()
    for g in (gq, go, gm):
        g.drain()
    for dz in range(4):
        sib_copy(dz).wait_send()
    for which in (0, 1):
        opp_copy(which).wait_send()
        for part in (0, 1):
            z_copy(which, part).wait_send()
    for step in range(1, 8):
        stat_copy(step).wait_send()
    msib_copy().wait_send()
    for step in (1, 2, 3):
        mz_copy(step).wait_send()
    own_out.wait()
    for step in range(1, 16):
        out_wait(step)
        out_copy(step).wait_send()


def per_device(
    tokens,
    grid_sizes,
    owners,
    ln_gain,
    ln_bias,
    w_qkv,
    w_out,
    layer_scale,
    merge_gain,
    merge_bias,
    w_merge,
):
    quarter = HEAD_DIM // 4
    lanes = jnp.arange(HEAD_DIM, dtype=jnp.int32) % quarter
    freqs = 100.0 ** (-lanes.astype(F32) / quarter)
    wq = w_qkv.reshape(2, 128, 3, 2, 256).transpose(3, 0, 1, 2, 4).reshape(2, 2, 128, 768)
    wo = w_out.reshape(2, 2, 128, 256)
    wm = w_merge.reshape(2, 2, 256, 256)

    any_space = pl.BlockSpec(memory_space=pl.ANY)
    vmem = pl.BlockSpec(memory_space=pltpu.VMEM)
    dma = pltpu.SemaphoreType.DMA
    out = pl.pallas_call(
        kernel,
        out_shape=jax.ShapeDtypeStruct((16, 32, 256), BF16),
        in_specs=[any_space] * 4 + [vmem] * 6 + [pl.BlockSpec(memory_space=pltpu.SMEM), vmem],
        out_specs=any_space,
        scratch_shapes=[
            pltpu.VMEM((2, 16, 2, 128, 768), BF16),
            pltpu.VMEM((2, 16, 2, 128, 256), BF16),
            pltpu.VMEM((2, 16, 2, 256, 256), BF16),
            pltpu.VMEM((1024, 4096), BF16),
            pltpu.VMEM((2, 1024, 768), F32),
            pltpu.VMEM((1024, 512), BF16),
            pltpu.VMEM((1024, 512), BF16),
            pltpu.VMEM((1024, 512), BF16),
            pltpu.VMEM((1024, 512), BF16),
            pltpu.VMEM((1024, 512), BF16),
            pltpu.VMEM((1024, 512), BF16),
            pltpu.VMEM((1024, 128), F32),
            pltpu.VMEM((1024, 128), F32),
            pltpu.VMEM((1024, 128), jnp.int32),
            pltpu.VMEM((256, 128), jnp.int32),
            pltpu.VMEM((1, 256), jnp.int32),
            pltpu.VMEM((4, 1024, 512), BF16),
            pltpu.VMEM((512, 512), BF16),
            pltpu.VMEM((512, 512), BF16),
            pltpu.VMEM((1024, 512), BF16),
            pltpu.VMEM((1024, 512), BF16),
            pltpu.VMEM((8, 8, 256), F32),
            pltpu.VMEM((2, 4, 256, 256), BF16),
            pltpu.VMEM((4, 256, 256), BF16),
            pltpu.VMEM((3, 256, 256), BF16),
            pltpu.VMEM((16, 32, 256), BF16),
            dma((2, 20)),
            dma((2, 20)),
            dma((2, 20)),
            dma((2, 20)),
            dma((2, 20)),
            dma((2, 20)),
            dma((10,)),
            dma((2,)),
            dma((2,)),
            dma((4,)),
            dma((4,)),
            dma((2,)),
            dma((2,)),
            dma((2, 2)),
            dma((2, 2)),
            dma((8,)),
            dma((8,)),
            dma,
            dma,
            dma((3,)),
            dma((3,)),
            dma((16,)),
            dma((16,)),
        ],
        compiler_params=pltpu.CompilerParams(
            collective_id=0, has_side_effects=True, vmem_limit_bytes=63 * 2**20
        ),
    )(
        tokens,
        wq,
        wo,
        wm,
        ln_gain[None],
        ln_bias[None],
        layer_scale[None],
        merge_gain,
        merge_bias,
        freqs[None],
        grid_sizes,
        owners.reshape(16, 256),
    )
    return out[:, :24].reshape(384, 256)


def solution(mesh):
    return jax.shard_map(
        per_device,
        mesh=mesh,
        in_specs=(
            P("rows", None),
            P(),
            P(),
            P(),
            P(),
            P("rows", None, "tensor"),
            P("tensor", "rows"),
            P(),
            P(),
            P(),
            P(None, "rows", "tensor"),
        ),
        out_specs=P("rows", "tensor"),
        check_vma=False,
    )
```

```python
import functools
import math

import jax
import jax.numpy as jnp
from jax import lax
from jax.experimental import pallas as pl
from jax.experimental.pallas import tpu as pltpu
from jax.sharding import PartitionSpec as P

MESH = pl.DeviceIdType.MESH
F32 = jnp.float32
BF16 = jnp.bfloat16
HEAD_DIM = 128
PREFIX = 5


class Gather:
    def __init__(self, src, region, send, recv, place):
        self.src, self.region, self.send, self.recv_sem = src, region, send, recv
        self.y, self.x, self.t = place
        table = [
            ((0, 0), None, (1, 0)),
            ((0, 0), None, (-1, 0)),
            ((0, 0), None, (0, 1)),
            ((0, 0), None, (0, -1)),
            ((-1, 0), 0, (1, 0)),
            ((1, 0), 1, (-1, 0)),
            ((-1, 0), None, (0, 1)),
            ((-1, 0), None, (0, -1)),
            ((1, 0), None, (0, 1)),
            ((1, 0), None, (0, -1)),
            ((2, 0), None, (0, 1)),
            ((2, 0), None, (0, -1)),
        ]
        for first in (0, -1, 1, 2):
            table.append(((first, -1), 0, (0, 1)))
            table.append(((first, 1), 1, (0, -1)))
        self.table = table

    def slot(self, half, first, second):
        dx, dy = (first, second) if half == 0 else (second, first)
        return lax.rem(self.y + (dy % 4), 4) * 4 + lax.rem(self.x + (dx % 4), 4)

    def copy(self, half, i):
        (first, second), part, to = self.table[i]
        slot = self.slot(half, first, second)
        dst = self.region(half, slot, part)
        src = self.src(half) if self.src is not None and i < 4 else dst
        return pltpu.make_async_remote_copy(
            src_ref=src,
            dst_ref=dst,
            send_sem=self.send.at[half, i],
            recv_sem=self.recv_sem.at[half, i],
            device_id=(self.slot(half, *to), self.t),
            device_id_type=MESH,
        )

    def start(self, *which):
        for i in which:
            for half in (0, 1):
                self.copy(half, i).start()

    def recv(self, *which):
        for i in which:
            for half in (0, 1):
                self.copy(half, i).wait_recv()

    def r1(self):
        self.start(0, 1, 2, 3)

    def r2(self):
        self.recv(0, 1)
        self.start(4, 5, 6, 7, 8, 9)

    def r3(self):
        self.recv(4, 5)
        self.start(10, 11)

    def r4a(self):
        self.recv(2, 3)
        self.start(12, 13)

    def r4b(self):
        self.recv(6, 7, 8, 9)
        self.start(14, 15, 16, 17)

    def r4c(self):
        self.recv(10, 11)
        self.start(18, 19)

    def finish(self):
        self.recv(12, 13, 14, 15, 16, 17, 18, 19)

    def drain(self):
        for i in range(20):
            for half in (0, 1):
                self.copy(half, i).wait_send()


def dot(a, b):
    return jnp.dot(a, b, preferred_element_type=F32)


def kernel(
    tokens,
    wq,
    wo,
    wm,
    ln_gain,
    ln_bias,
    scale,
    merge_gain,
    merge_bias,
    grid_ref,
    own_ref,
    out,
    bufq,
    bufo,
    bufm,
    normed,
    acc,
    qb,
    kb,
    vb,
    att,
    tok,
    tokp,
    cos_ref,
    sin_ref,
    src_ref,
    segq_ref,
    pos_ref,
    wo_in,
    scale_own,
    gain_own,
    bias_own,
    fromsib,
    oppa,
    oppb,
    zprev,
    znext,
    stats,
    mpart,
    msib,
    mz,
    obuf,
    sq,
    rq,
    so,
    ro,
    sm,
    rm,
    local,
    sperm,
    rperm,
    ssib,
    rsib,
    sopp,
    ropp,
    sz,
    rz,
    sstat,
    rstat,
    smsib,
    rmsib,
    smz,
    rmz,
    sout,
    rout,
):
    r = lax.axis_index("rows")
    t = lax.axis_index("tensor")
    y, x = lax.div(r, 4), lax.rem(r, 4)
    z, c = lax.div(t, 2), lax.rem(t, 2)
    place = (y, x, t)
    tiles = 4
    rows_tile = 256

    def zdev(offset, core=None):
        return lax.rem(z + offset % 4, 4) * 2 + (c if core is None else core)

    sibling = z * 2 + (1 - c)
    barrier = pltpu.get_barrier_semaphore()
    for step in range(1, 16):
        pl.semaphore_signal(
            barrier, inc=1, device_id=(lax.rem(r + step, 16), t), device_id_type=MESH
        )
    for step in range(1, 8):
        pl.semaphore_signal(
            barrier, inc=1, device_id=(r, lax.rem(t + step, 8)), device_id_type=MESH
        )
    pl.semaphore_wait(barrier, 22)

    def src_q(half):
        return wq.at[:, :, pl.ds(256 * half, 256)]

    def region_q(half, slot, part):
        if part is None:
            return bufq.at[half, slot]
        return bufq.at[half, slot, :, pl.ds(128 * part, 128)]

    def region_o(half, slot, part):
        if part is None:
            return bufo.at[pl.ds(4 * half, 4), slot]
        return bufo.at[pl.ds(4 * half + 2 * part, 2), slot]

    def region_m(half, slot, part):
        return bufm.at[half, slot] if part is None else bufm.at[half, slot, part]

    gq = Gather(src_q, region_q, sq, rq, place)
    go = Gather(None, region_o, so, ro, place)
    gm = Gather(None, region_m, sm, rm, place)

    gq.r1()

    def deal_piece(to):
        return wm.at[:, :, pl.ds(pl.multiple_of(to * 32, 32), 32), :]

    def deal_place(come):
        return bufm.at[:, r, :, :, pl.ds(pl.multiple_of(come * 256, 256), 256)]

    def deal_copy(step):
        to = lax.rem(t + step, 8)
        return pltpu.make_async_remote_copy(
            src_ref=deal_piece(to),
            dst_ref=deal_place(t),
            send_sem=sperm.at[step],
            recv_sem=rperm.at[step],
            device_id=(r, to),
            device_id_type=MESH,
        )

    def deal_wait(step):
        come = lax.rem(t + 8 - step, 8)
        pltpu.make_async_remote_copy(
            src_ref=deal_piece(come),
            dst_ref=deal_place(come),
            send_sem=sperm.at[step],
            recv_sem=rperm.at[step],
            device_id=(r, come),
            device_id_type=MESH,
        ).wait_recv()

    own_deal = pltpu.make_async_copy(deal_piece(t), deal_place(t), local.at[6])

    chunk = 256

    def tok_copy(i):
        rows = pl.ds(i * chunk, chunk)
        return pltpu.make_async_copy(tokens.at[rows], normed.at[rows], local.at[i])

    for i in range(4):
        tok_copy(i).start()
    own_q = [pltpu.make_async_copy(src_q(h), bufq.at[h, r], local.at[4 + h]) for h in (0, 1)]
    own_wo = pltpu.make_async_copy(wo, wo_in, local.at[7])
    for copy in own_q + [own_wo, own_deal]:
        copy.start()
    for step in range(1, 8):
        deal_copy(step).start()

    feature_tile = lax.div(t, 4) * 128

    def own_features(load):
        tiles_out = []
        for j in range(4):
            taken = None
            for q in range(4):
                v = load(pl.ds(pl.multiple_of(256 * (4 * j + q) + feature_tile, 128), 128))
                v = pltpu.roll(v, lax.rem(32 * q + 128 - 32 * lax.rem(t, 4), 128), 1)
                if q:
                    at = lax.broadcasted_iota(jnp.int32, v.shape, 1)
                    v = jnp.where(at >= 32 * q, v, taken)
                taken = v
            tiles_out.append(taken)
        return jnp.concatenate(tiles_out, axis=1)

    def norm_chunk(i):
        tok_copy(i).wait()
        step = 16

        def body(j, carry):
            at = pl.ds(pl.multiple_of(i * chunk + j * step, step), step)
            tok[at, :] = own_features(lambda cols: normed[at, cols].astype(F32)).astype(BF16)
            v = normed[at, :].astype(F32)
            mean = jnp.mean(v, axis=-1, keepdims=True)
            v = v - mean
            var = jnp.mean(v * v, axis=-1, keepdims=True)
            v = v * lax.rsqrt(var + 1e-6) * ln_gain[...] + ln_bias[...]
            normed[at, :] = v.astype(BF16)
            return carry

        lax.fori_loop(0, chunk // step, body, 0)

    grid = grid_ref[r]
    heights = [grid[i : i + 1, 0:1] for i in range(4)]
    widths = [grid[i : i + 1, 1:2] for i in range(4)]
    starts, merged_starts = [jnp.zeros((1, 1), jnp.int32)], [jnp.zeros((1, 1), jnp.int32)]
    for h, w in zip(heights, widths):
        starts.append(starts[-1] + PREFIX + h * w)
        merged_starts.append(merged_starts[-1] + ((h * w).astype(F32) * 0.25).astype(jnp.int32))
    lane = lax.broadcasted_iota(jnp.int32, (rows_tile, HEAD_DIM), 1)
    low = lax.rem(lane, 64) < 32

    freqs = jnp.exp2(lax.rem(lane[0:1, :], 32).astype(F32) * (-math.log2(100.0) / 32))

    def choose(at, edges, values):
        chosen = jnp.zeros(at.shape, jnp.int32) + values[0]
        for edge, value in zip(edges[1:4], values[1:4]):
            chosen = jnp.where(at >= edge, value, chosen)
        return chosen

    def tables(i, carry):
        at = pl.ds(pl.multiple_of(i * rows_tile, rows_tile), rows_tile)
        pos = lax.broadcasted_iota(jnp.int32, (rows_tile, HEAD_DIM), 0) + i * rows_tile
        local_pos = pos - choose(pos, starts, starts) - PREFIX
        patch = (local_pos >= 0) & (pos < starts[4])
        flat = jnp.where(patch, local_pos, 0).astype(F32)
        width = choose(pos, starts, widths).astype(F32)
        row = jnp.floor((flat + 0.5) / width)
        angle = jnp.where(lane < 64, row, flat - row * width) * freqs
        cos_ref[at, :] = jnp.cos(angle)
        sine = jnp.sin(angle)
        sin_ref[at, :] = jnp.where(low, -sine, sine)
        return carry

    def slots_layout():
        m = lax.broadcasted_iota(jnp.int32, (rows_tile, HEAD_DIM), 0)
        live = m < merged_starts[4]
        width = choose(m, merged_starts, widths).astype(F32)
        first = choose(m, merged_starts, starts).astype(F32) + PREFIX
        offset = (m - choose(m, merged_starts, merged_starts)).astype(F32)
        row = jnp.floor((offset + 0.5) / (0.5 * width))
        corner = first + (2.0 * row) * width + 2.0 * (offset - row * (0.5 * width))
        for k in range(4):
            source = corner + width * float(k // 2) + float(k % 2)
            src_ref[k * rows_tile : (k + 1) * rows_tile, :] = jnp.where(live, source, 0.0).astype(
                jnp.int32
            )
        segq_ref[...] = jnp.where(live, choose(m, merged_starts, [0, 1, 2, 3]), 0)

        own_row = own_ref[...]
        own_col = jnp.broadcast_to(own_row.astype(F32), (HEAD_DIM, 256)).T[:, 0:1]
        before = lax.broadcasted_iota(jnp.int32, (256, 256), 0) < lax.broadcasted_iota(
            jnp.int32, (256, 256), 1
        )
        hit = before & (own_col == own_row.astype(F32))
        rank = jnp.sum(jnp.where(hit, 1.0, 0.0), axis=0, keepdims=True).astype(jnp.int32)
        live_row = lax.broadcasted_iota(jnp.int32, (1, 256), 1) < merged_starts[4]
        pos_ref[...] = jnp.where(live_row, own_row * 32 + rank, -1)

    key_pos = lax.broadcasted_iota(jnp.int32, (1, 1024), 1)
    segk = jnp.zeros((1, 1024), jnp.int32)
    for edge in starts[1:]:
        segk = segk + (key_pos >= edge).astype(jnp.int32)

    def project(slots, first=False):
        for half in (0, 1):
            where = [gq.slot(half, *s) for s in slots]

            def body(i, carry, half=half, where=where):
                out_cols = pl.ds(pl.multiple_of(i * 256, 256), 256)
                total = None
                for w in where:
                    cols = pl.ds(pl.multiple_of(w * 256, 256), 256)
                    term = dot(normed[:, cols], bufq[half, w, i])
                    total = term if total is None else total + term
                if first:
                    acc[half, :, out_cols] = total
                else:
                    acc[half, :, out_cols] += total
                return carry

            lax.fori_loop(0, 3, body, 0)

    for i in range(3):
        norm_chunk(i)
    for copy in own_q:
        copy.wait()
    gq.r2()
    norm_chunk(3)
    gq.r4a()
    project([(0, 0), (-1, 0), (1, 0)], first=True)
    project([(0, -1), (0, 1)])
    gq.r3()
    project([(2, 0)])
    lax.fori_loop(0, tiles, tables, 0)
    slots_layout()
    own_wo.wait()
    turned = wo_in[...].astype(F32).T.astype(BF16)
    for i in range(8):
        bufo[i, r] = turned[32 * i : 32 * i + 32, :]
    scale_own[...] = own_features(lambda cols: scale[:, cols])
    gain_own[...] = own_features(lambda cols: merge_gain[:, cols])
    bias_own[...] = own_features(lambda cols: merge_bias[:, cols])
    gq.r4b()
    go.r1()
    project([(-1, -1), (-1, 1), (1, -1), (1, 1)])
    gq.r4c()
    project([(2, -1), (2, 1)])
    gq.recv(12, 13, 14, 15)
    project([(0, 2), (-1, 2)])
    go.r2()
    go.r4a()
    gq.recv(16, 17, 18, 19)
    project([(1, 2), (2, 2)])
    go.r3()

    def rotate(i, carry):
        at = pl.ds(pl.multiple_of(i * rows_tile, rows_tile), rows_tile)
        cosine, sine = cos_ref[at, :], sin_ref[at, :]
        for head in range(4):
            half, inner = divmod(head, 2)
            for dst, base in ((qb, 0), (kb, 256)):
                v = acc[half, at, base + inner * 128 : base + inner * 128 + 128]
                partner = jnp.where(low, pltpu.roll(v, 96, 1), pltpu.roll(v, 32, 1))
                dst[at, head * 128 : head * 128 + 128] = (v * cosine + partner * sine).astype(BF16)
            vb[at, head * 128 : head * 128 + 128] = acc[
                half, at, 512 + inner * 128 : 512 + inner * 128 + 128
            ].astype(BF16)
        return carry

    lax.fori_loop(0, tiles, rotate, 0)

    factor = HEAD_DIM ** (-0.5) / math.log(2.0)

    def attend(k):
        at = slice(k * rows_tile, (k + 1) * rows_tile)
        pick = (
            lax.broadcasted_iota(jnp.int32, (rows_tile, 1024), 1) == src_ref[at, 0:1]
        ).astype(BF16)
        att[at, :] = dot(pick, qb[...]).astype(BF16)
        tokp[at, :] = dot(pick, tok[...]).astype(BF16)

        def body(head, carry):
            cols = pl.ds(pl.multiple_of(head * 128, 128), 128)
            s = lax.dot_general(
                att[at, cols], kb[:, cols], (((1,), (1,)), ((), ())), preferred_element_type=F32
            )
            s = jnp.where(segq_ref[:, 0:1] == segk, s, -jnp.inf)
            top = jnp.max(s, axis=-1, keepdims=True)
            e = jnp.exp2((s - top) * factor)
            total = jnp.sum(e, axis=-1, keepdims=True)
            o = dot(e.astype(BF16), vb[:, cols])
            att[at, cols] = (o / total).astype(BF16)
            return carry

        lax.fori_loop(0, 4, body, 0)

    def out_project(to):
        def body(j, carry):
            weight = bufo[to, pl.ds(j * 8, 8)].reshape(256, 512)
            total = lax.dot_general(
                att[...], weight, (((1,), (1,)), ((), ())), preferred_element_type=F32
            )
            cols = pl.ds(pl.multiple_of(to * 512 + j * 256, 256), 256)
            normed[:, cols] = total.astype(BF16)
            return carry

        lax.fori_loop(0, 2, body, 0)

    def chunk_of(tensor, lo=0, rows=1024):
        return normed.at[pl.ds(lo, rows), pl.ds(pl.multiple_of(tensor * 512, 512), 512)]

    def sib_copy(dz):
        return pltpu.make_async_remote_copy(
            src_ref=chunk_of(zdev(dz, 1 - c)),
            dst_ref=fromsib.at[dz % 4],
            send_sem=ssib.at[dz % 4],
            recv_sem=rsib.at[dz % 4],
            device_id=(r, sibling),
            device_id_type=MESH,
        )

    def opp_copy(which):
        return pltpu.make_async_remote_copy(
            src_ref=chunk_of(zdev(2), 512 * which, 512),
            dst_ref=(oppa, oppb)[which],
            send_sem=sopp.at[which],
            recv_sem=ropp.at[which],
            device_id=(r, zdev(1 if which == 0 else -1)),
            device_id_type=MESH,
        )

    def z_copy(which, part):
        to = zdev(1 if which == 0 else -1)
        return pltpu.make_async_remote_copy(
            src_ref=chunk_of(to, 512 * part, 512),
            dst_ref=(zprev, znext)[which].at[pl.ds(512 * part, 512)],
            send_sem=sz.at[which, part],
            recv_sem=rz.at[which, part],
            device_id=(r, to),
            device_id_type=MESH,
        )

    def partial(dz):
        out_project(zdev(dz, 1 - c))
        sib_copy(dz).start()
        out_project(zdev(dz))

    def add_sibling(dz):
        sib_copy(dz).wait_recv()

        def body(i, carry):
            ref = chunk_of(zdev(dz), pl.multiple_of(i * 256, 256), 256)
            other = fromsib[dz % 4, pl.ds(pl.multiple_of(i * 256, 256), 256), :]
            ref[...] = (ref[...].astype(F32) + other.astype(F32)).astype(BF16)
            return carry

        lax.fori_loop(0, 4, body, 0)

    def pass_on(which):
        opp_copy(which).wait_recv()
        for i in (0, 1):
            ref = chunk_of(zdev(1 if which == 0 else -1), 512 * which + 256 * i, 256)
            other = (oppa, oppb)[which][256 * i : 256 * i + 256, :]
            ref[...] = (ref[...].astype(F32) + other.astype(F32)).astype(BF16)
        z_copy(which, which).start()

    sums = []

    def finish_rows(k):
        at = slice(k * rows_tile, (k + 1) * rows_tile)
        total = (
            chunk_of(t, k * rows_tile, rows_tile)[...].astype(F32)
            + fromsib[0, at, :].astype(F32)
            + zprev[at, :].astype(F32)
            + znext[at, :].astype(F32)
        )
        res = tokp[at, :].astype(F32) + scale_own[...] * total
        acc[0, at, 0:512] = res
        sums.append(jnp.sum(res, axis=-1, keepdims=True))

    go.r4b()
    attend(0)
    go.r4c()
    own_deal.wait()
    for step in range(1, 8):
        deal_wait(step)
    gm.r1()
    attend(1)
    attend(2)
    attend(3)
    go.finish()
    partial(2)
    gm.r2()
    partial(1)
    add_sibling(2)
    opp_copy(0).start()
    opp_copy(1).start()
    partial(-1)
    add_sibling(1)
    z_copy(0, 1).start()
    gm.r4a()
    add_sibling(-1)
    z_copy(1, 0).start()
    partial(0)
    gm.r3()
    pass_on(0)
    pass_on(1)
    gm.r4b()
    sib_copy(0).wait_recv()
    z_copy(0, 1).wait_recv()
    z_copy(1, 1).wait_recv()
    z_copy(0, 0).wait_recv()
    z_copy(1, 0).wait_recv()
    gm.r4c()
    for k in range(4):
        finish_rows(k)

    mean_l = (sums[0] + sums[1] + sums[2] + sums[3]) * (1.0 / 2048)
    m2 = None
    for k in range(4):
        d = acc[0, k * 256 : (k + 1) * 256, 0:512] - mean_l
        term = jnp.sum(d * d, axis=-1, keepdims=True)
        m2 = term if m2 is None else m2 + term
    packed = jnp.where(lane == 0, mean_l, m2)
    stats[0] = packed.T[0:8, :]

    def stat_copy(step):
        return pltpu.make_async_remote_copy(
            src_ref=stats.at[0],
            dst_ref=stats.at[step],
            send_sem=sstat.at[step],
            recv_sem=rstat.at[step],
            device_id=(r, lax.rem(t + step, 8)),
            device_id_type=MESH,
        )

    for step in range(1, 8):
        stat_copy(step).start()
    gm.finish()
    for step in range(1, 8):
        stat_copy(step).wait_recv()
    means = [stats[i][0:1, :] for i in range(8)]
    m2s = [stats[i][1:2, :] for i in range(8)]
    mean = functools.reduce(lambda a, b: a + b, means) * 0.125
    total2 = functools.reduce(lambda a, b: a + b, m2s)
    for m in means:
        total2 = total2 + 2048.0 * (m - mean) * (m - mean)
    rs = lax.rsqrt(total2 * (1.0 / 16384) + 1e-6)
    row = lax.broadcasted_iota(jnp.int32, (128, 256), 0)
    back = jnp.where(row == 0, mean, rs).T
    mean_c, rs_c = back[:, 0:1], back[:, 1:2]
    for k in range(4):
        at = slice(k * rows_tile, (k + 1) * rows_tile)
        v = (acc[0, at, 0:512] - mean_c) * rs_c
        v = v * gain_own[k : k + 1, :] + bias_own[k : k + 1, :]
        att[at, :] = v.astype(BF16)

    def merge_project(core):
        def body(zz, carry):
            total = None
            for k in range(4):
                for j in (0, 1):
                    cols = pl.ds(pl.multiple_of((zz * 2 + core) * 256, 256), 256)
                    term = dot(
                        att[k * 256 : (k + 1) * 256, j * 256 : j * 256 + 256],
                        bufm[k // 2, 8 * j : 8 * j + 8, k % 2, :, cols].reshape(256, 256),
                    )
                    total = term if total is None else total + term
            mpart[core, zz] = total.astype(BF16)
            return carry

        lax.fori_loop(0, 4, body, 0)

    def msib_copy():
        return pltpu.make_async_remote_copy(
            src_ref=mpart.at[1 - c],
            dst_ref=msib,
            send_sem=smsib,
            recv_sem=rmsib,
            device_id=(r, sibling),
            device_id_type=MESH,
        )

    merge_project(1 - c)
    msib_copy().start()
    merge_project(c)
    msib_copy().wait_recv()

    def mz_copy(step):
        zz = lax.rem(z + step, 4)
        return pltpu.make_async_remote_copy(
            src_ref=mpart.at[c, zz],
            dst_ref=mz.at[step - 1],
            send_sem=smz.at[step - 1],
            recv_sem=rmz.at[step - 1],
            device_id=(r, zz * 2 + c),
            device_id_type=MESH,
        )

    for step in (2, 1, 3):
        zz = lax.rem(z + step, 4)
        mpart[c, zz] = (mpart[c, zz].astype(F32) + msib[zz].astype(F32)).astype(BF16)
        mz_copy(step).start()
    merged = mpart[c, z].astype(F32) + msib[z].astype(F32)
    for step in (1, 3, 2):
        mz_copy(step).wait_recv()
        merged = merged + mz[step - 1].astype(F32)
    merged = merged.astype(BF16)

    place_row = (lax.broadcasted_iota(jnp.int32, (512, 256), 0) == pos_ref[...]).astype(BF16)
    obuf[...] = dot(place_row, merged).astype(BF16).reshape(16, 32, 256)

    def out_copy(step):
        to = lax.rem(r + step, 16)
        return pltpu.make_async_remote_copy(
            src_ref=obuf.at[to],
            dst_ref=out.at[r],
            send_sem=sout.at[step],
            recv_sem=rout.at[step],
            device_id=(to, t),
            device_id_type=MESH,
        )

    def out_wait(step):
        come = lax.rem(r + 16 - step, 16)
        pltpu.make_async_remote_copy(
            src_ref=obuf.at[come],
            dst_ref=out.at[come],
            send_sem=sout.at[step],
            recv_sem=rout.at[step],
            device_id=(come, t),
            device_id_type=MESH,
        ).wait_recv()

    own_out = pltpu.make_async_copy(obuf.at[r], out.at[r], local.at[9])
    for step in range(1, 16):
        out_copy(step).start()
    own_out.start()

    for step in range(1, 8):
        deal_copy(step).wait_send()
    for g in (gq, go, gm):
        g.drain()
    for dz in range(4):
        sib_copy(dz).wait_send()
    for which in (0, 1):
        opp_copy(which).wait_send()
        for part in (0, 1):
            z_copy(which, part).wait_send()
    for step in range(1, 8):
        stat_copy(step).wait_send()
    msib_copy().wait_send()
    for step in (1, 2, 3):
        mz_copy(step).wait_send()
    own_out.wait()
    for step in range(1, 16):
        out_wait(step)
        out_copy(step).wait_send()


def per_device(
    tokens,
    grid_sizes,
    owners,
    ln_gain,
    ln_bias,
    w_qkv,
    w_out,
    layer_scale,
    merge_gain,
    merge_bias,
    w_merge,
):
    own_row = lax.dynamic_slice_in_dim(owners, lax.axis_index("rows") * 256, 256).reshape(1, 256)
    wq = w_qkv.transpose(1, 0, 2)
    wm = w_merge.reshape(2, 2, 256, 256)

    any_space = pl.BlockSpec(memory_space=pl.ANY)
    vmem = pl.BlockSpec(memory_space=pltpu.VMEM)
    dma = pltpu.SemaphoreType.DMA
    out = pl.pallas_call(
        kernel,
        out_shape=jax.ShapeDtypeStruct((16, 32, 256), BF16),
        in_specs=[any_space] * 4 + [vmem] * 7,
        out_specs=any_space,
        scratch_shapes=[
            pltpu.VMEM((2, 16, 3, 256, 256), BF16),
            pltpu.VMEM((8, 16, 32, 512), BF16),
            pltpu.VMEM((2, 16, 2, 32, 2048), BF16),
            pltpu.VMEM((1024, 4096), BF16),
            pltpu.VMEM((2, 1024, 768), F32),
            pltpu.VMEM((1024, 512), BF16),
            pltpu.VMEM((1024, 512), BF16),
            pltpu.VMEM((1024, 512), BF16),
            pltpu.VMEM((1024, 512), BF16),
            pltpu.VMEM((1024, 512), BF16),
            pltpu.VMEM((1024, 512), BF16),
            pltpu.VMEM((1024, 128), F32),
            pltpu.VMEM((1024, 128), F32),
            pltpu.VMEM((1024, 128), jnp.int32),
            pltpu.VMEM((256, 128), jnp.int32),
            pltpu.VMEM((1, 256), jnp.int32),
            pltpu.VMEM((512, 256), BF16),
            pltpu.VMEM((1, 512), F32),
            pltpu.VMEM((4, 512), F32),
            pltpu.VMEM((4, 512), F32),
            pltpu.VMEM((4, 1024, 512), BF16),
            pltpu.VMEM((512, 512), BF16),
            pltpu.VMEM((512, 512), BF16),
            pltpu.VMEM((1024, 512), BF16),
            pltpu.VMEM((1024, 512), BF16),
            pltpu.VMEM((8, 8, 256), F32),
            pltpu.VMEM((2, 4, 256, 256), BF16),
            pltpu.VMEM((4, 256, 256), BF16),
            pltpu.VMEM((3, 256, 256), BF16),
            pltpu.VMEM((16, 32, 256), BF16),
            dma((2, 20)),
            dma((2, 20)),
            dma((2, 20)),
            dma((2, 20)),
            dma((2, 20)),
            dma((2, 20)),
            dma((10,)),
            dma((8,)),
            dma((8,)),
            dma((4,)),
            dma((4,)),
            dma((2,)),
            dma((2,)),
            dma((2, 2)),
            dma((2, 2)),
            dma((8,)),
            dma((8,)),
            dma,
            dma,
            dma((3,)),
            dma((3,)),
            dma((16,)),
            dma((16,)),
        ],
        compiler_params=pltpu.CompilerParams(
            collective_id=0, has_side_effects=True, vmem_limit_bytes=63 * 2**20
        ),
    )(
        tokens,
        wq,
        w_out,
        wm,
        ln_gain[None],
        ln_bias[None],
        layer_scale[None],
        merge_gain,
        merge_bias,
        grid_sizes,
        own_row,
    )
    return out[:, :24].reshape(384, 256)


def solution(mesh):
    return jax.shard_map(
        per_device,
        mesh=mesh,
        in_specs=(
            P("rows", None),
            P(),
            P(),
            P(),
            P(),
            P("rows", None, "tensor"),
            P("tensor", "rows"),
            P(),
            P(),
            P(),
            P(None, "rows", "tensor"),
        ),
        out_specs=P("rows", "tensor"),
        check_vma=False,
    )
```

```python
import functools
import math

import jax
import jax.numpy as jnp
from jax import lax
from jax.experimental import pallas as pl
from jax.experimental.pallas import tpu as pltpu
from jax.sharding import PartitionSpec as P

MESH = pl.DeviceIdType.MESH
F32 = jnp.float32
BF16 = jnp.bfloat16
HEAD_DIM = 128
PREFIX = 5


class Gather:
    def __init__(self, src, region, send, recv, place):
        self.src, self.region, self.send, self.recv_sem = src, region, send, recv
        self.y, self.x, self.t = place
        table = [
            ((0, 0), None, (1, 0)),
            ((0, 0), None, (-1, 0)),
            ((0, 0), None, (0, 1)),
            ((0, 0), None, (0, -1)),
            ((-1, 0), 0, (1, 0)),
            ((1, 0), 1, (-1, 0)),
            ((-1, 0), None, (0, 1)),
            ((-1, 0), None, (0, -1)),
            ((1, 0), None, (0, 1)),
            ((1, 0), None, (0, -1)),
            ((2, 0), None, (0, 1)),
            ((2, 0), None, (0, -1)),
        ]
        for first in (0, -1, 1, 2):
            table.append(((first, -1), 0, (0, 1)))
            table.append(((first, 1), 1, (0, -1)))
        self.table = table

    def slot(self, half, first, second):
        dx, dy = (first, second) if half == 0 else (second, first)
        return lax.rem(self.y + (dy % 4), 4) * 4 + lax.rem(self.x + (dx % 4), 4)

    def copy(self, half, i):
        (first, second), part, to = self.table[i]
        slot = self.slot(half, first, second)
        dst = self.region(half, slot, part)
        src = self.src(half) if self.src is not None and i < 4 else dst
        return pltpu.make_async_remote_copy(
            src_ref=src,
            dst_ref=dst,
            send_sem=self.send.at[half, i],
            recv_sem=self.recv_sem.at[half, i],
            device_id=(self.slot(half, *to), self.t),
            device_id_type=MESH,
        )

    def start(self, *which):
        for i in which:
            for half in (0, 1):
                self.copy(half, i).start()

    def recv(self, *which):
        for i in which:
            for half in (0, 1):
                self.copy(half, i).wait_recv()

    def r1(self):
        self.start(0, 1, 2, 3)

    def r2(self):
        self.recv(0, 1)
        self.start(4, 5, 6, 7, 8, 9)

    def r3(self):
        self.recv(4, 5)
        self.start(10, 11)

    def r4a(self):
        self.recv(2, 3)
        self.start(12, 13)

    def r4b(self):
        self.recv(6, 7, 8, 9)
        self.start(14, 15, 16, 17)

    def r4c(self):
        self.recv(10, 11)
        self.start(18, 19)

    def finish(self):
        self.recv(12, 13, 14, 15, 16, 17, 18, 19)

    def drain(self):
        for i in range(20):
            for half in (0, 1):
                self.copy(half, i).wait_send()


def dot(a, b):
    return jnp.dot(a, b, preferred_element_type=F32)


def kernel(
    tokens,
    wq,
    wo,
    wm,
    ln_gain,
    ln_bias,
    scale,
    merge_gain,
    merge_bias,
    grid_ref,
    own_ref,
    out,
    bufq,
    bufo,
    bufm,
    normed,
    acc,
    qb,
    kb,
    vb,
    att,
    tok,
    tokp,
    cos_ref,
    sin_ref,
    src_ref,
    segq_ref,
    pos_ref,
    wo_in,
    scale_own,
    gain_own,
    bias_own,
    fromsib,
    oppa,
    oppb,
    zprev,
    znext,
    stats,
    mpart,
    msib,
    mopp,
    mz,
    obuf,
    sq,
    rq,
    so,
    ro,
    sm,
    rm,
    local,
    sperm,
    rperm,
    ssib,
    rsib,
    sopp,
    ropp,
    sz,
    rz,
    sstat,
    rstat,
    smsib,
    rmsib,
    smopp,
    rmopp,
    smz,
    rmz,
    sout,
    rout,
):
    r = lax.axis_index("rows")
    t = lax.axis_index("tensor")
    y, x = lax.div(r, 4), lax.rem(r, 4)
    z, c = lax.div(t, 2), lax.rem(t, 2)
    place = (y, x, t)
    tiles = 4
    rows_tile = 256

    def zdev(offset, core=None):
        return lax.rem(z + offset % 4, 4) * 2 + (c if core is None else core)

    sibling = z * 2 + (1 - c)
    barrier = pltpu.get_barrier_semaphore()
    for step in range(1, 16):
        pl.semaphore_signal(
            barrier, inc=1, device_id=(lax.rem(r + step, 16), t), device_id_type=MESH
        )
    for step in range(1, 8):
        pl.semaphore_signal(
            barrier, inc=1, device_id=(r, lax.rem(t + step, 8)), device_id_type=MESH
        )
    pl.semaphore_wait(barrier, 22)

    def src_q(half):
        return wq.at[:, :, pl.ds(256 * half, 256)]

    def region_q(half, slot, part):
        if part is None:
            return bufq.at[half, slot]
        return bufq.at[half, slot, :, pl.ds(128 * part, 128)]

    def region_o(half, slot, part):
        if part is None:
            return bufo.at[pl.ds(4 * half, 4), slot]
        return bufo.at[pl.ds(4 * half + 2 * part, 2), slot]

    def region_m(half, slot, part):
        return bufm.at[half, slot] if part is None else bufm.at[half, slot, part]

    gq = Gather(src_q, region_q, sq, rq, place)
    go = Gather(None, region_o, so, ro, place)
    gm = Gather(None, region_m, sm, rm, place)

    gq.r1()

    def deal_piece(to):
        return wm.at[:, :, pl.ds(pl.multiple_of(to * 32, 32), 32), :]

    def deal_place(come):
        return bufm.at[:, r, :, :, pl.ds(pl.multiple_of(come * 256, 256), 256)]

    def deal_copy(step):
        to = lax.rem(t + step, 8)
        return pltpu.make_async_remote_copy(
            src_ref=deal_piece(to),
            dst_ref=deal_place(t),
            send_sem=sperm.at[step],
            recv_sem=rperm.at[step],
            device_id=(r, to),
            device_id_type=MESH,
        )

    def deal_wait(step):
        come = lax.rem(t + 8 - step, 8)
        pltpu.make_async_remote_copy(
            src_ref=deal_piece(come),
            dst_ref=deal_place(come),
            send_sem=sperm.at[step],
            recv_sem=rperm.at[step],
            device_id=(r, come),
            device_id_type=MESH,
        ).wait_recv()

    own_deal = pltpu.make_async_copy(deal_piece(t), deal_place(t), local.at[6])

    chunk = 256

    def tok_copy(i):
        rows = pl.ds(i * chunk, chunk)
        return pltpu.make_async_copy(tokens.at[rows], normed.at[rows], local.at[i])

    for i in range(4):
        tok_copy(i).start()
    own_q = [pltpu.make_async_copy(src_q(h), bufq.at[h, r], local.at[4 + h]) for h in (0, 1)]
    own_wo = pltpu.make_async_copy(wo, wo_in, local.at[7])
    for copy in own_q + [own_wo, own_deal]:
        copy.start()
    for step in range(1, 8):
        deal_copy(step).start()

    feature_tile = lax.div(t, 4) * 128

    def own_features(load):
        tiles_out = []
        for j in range(4):
            taken = None
            for q in range(4):
                v = load(pl.ds(pl.multiple_of(256 * (4 * j + q) + feature_tile, 128), 128))
                v = pltpu.roll(v, lax.rem(32 * q + 128 - 32 * lax.rem(t, 4), 128), 1)
                if q:
                    at = lax.broadcasted_iota(jnp.int32, v.shape, 1)
                    v = jnp.where(at >= 32 * q, v, taken)
                taken = v
            tiles_out.append(taken)
        return jnp.concatenate(tiles_out, axis=1)

    def norm_chunk(i):
        tok_copy(i).wait()
        step = 16

        def body(j, carry):
            at = pl.ds(pl.multiple_of(i * chunk + j * step, step), step)
            tok[at, :] = own_features(lambda cols: normed[at, cols].astype(F32)).astype(BF16)
            v = normed[at, :].astype(F32)
            mean = jnp.mean(v, axis=-1, keepdims=True)
            v = v - mean
            var = jnp.mean(v * v, axis=-1, keepdims=True)
            v = v * lax.rsqrt(var + 1e-6) * ln_gain[...] + ln_bias[...]
            normed[at, :] = v.astype(BF16)
            return carry

        lax.fori_loop(0, chunk // step, body, 0)

    grid = grid_ref[...]
    heights = [grid[:, 2 * i : 2 * i + 1] for i in range(4)]
    widths = [grid[:, 2 * i + 1 : 2 * i + 2] for i in range(4)]
    starts, merged_starts = [jnp.zeros((1, 1), jnp.int32)], [jnp.zeros((1, 1), jnp.int32)]
    for h, w in zip(heights, widths):
        starts.append(starts[-1] + PREFIX + h * w)
        merged_starts.append(merged_starts[-1] + ((h * w).astype(F32) * 0.25).astype(jnp.int32))
    lane = lax.broadcasted_iota(jnp.int32, (rows_tile, HEAD_DIM), 1)
    low = lax.rem(lane, 64) < 32

    freqs = jnp.exp2(lax.rem(lane[0:1, :], 32).astype(F32) * (-math.log2(100.0) / 32))

    def choose(at, edges, values):
        chosen = jnp.zeros(at.shape, jnp.int32) + values[0]
        for edge, value in zip(edges[1:4], values[1:4]):
            chosen = jnp.where(at >= edge, value, chosen)
        return chosen

    def tables(i, carry):
        at = pl.ds(pl.multiple_of(i * rows_tile, rows_tile), rows_tile)
        pos = lax.broadcasted_iota(jnp.int32, (rows_tile, HEAD_DIM), 0) + i * rows_tile
        local_pos = pos - choose(pos, starts, starts) - PREFIX
        patch = (local_pos >= 0) & (pos < starts[4])
        flat = jnp.where(patch, local_pos, 0).astype(F32)
        width = choose(pos, starts, widths).astype(F32)
        row = jnp.floor((flat + 0.5) / width)
        angle = jnp.where(lane < 64, row, flat - row * width) * freqs
        cos_ref[at, :] = jnp.cos(angle)
        sine = jnp.sin(angle)
        sin_ref[at, :] = jnp.where(low, -sine, sine)
        return carry

    def slots_layout():
        m = lax.broadcasted_iota(jnp.int32, (rows_tile, HEAD_DIM), 0)
        live = m < merged_starts[4]
        width = choose(m, merged_starts, widths).astype(F32)
        first = choose(m, merged_starts, starts).astype(F32) + PREFIX
        offset = (m - choose(m, merged_starts, merged_starts)).astype(F32)
        row = jnp.floor((offset + 0.5) / (0.5 * width))
        corner = first + (2.0 * row) * width + 2.0 * (offset - row * (0.5 * width))
        for k in range(4):
            source = corner + width * float(k // 2) + float(k % 2)
            src_ref[k * rows_tile : (k + 1) * rows_tile, :] = jnp.where(live, source, 0.0).astype(
                jnp.int32
            )
        segq_ref[...] = jnp.where(live, choose(m, merged_starts, [0, 1, 2, 3]), 0)

        own_row = own_ref[...]
        own_col = jnp.broadcast_to(own_row.astype(F32), (HEAD_DIM, 256)).T[:, 0:1]
        before = lax.broadcasted_iota(jnp.int32, (256, 256), 0) < lax.broadcasted_iota(
            jnp.int32, (256, 256), 1
        )
        hit = before & (own_col == own_row.astype(F32))
        rank = jnp.sum(jnp.where(hit, 1.0, 0.0), axis=0, keepdims=True).astype(jnp.int32)
        live_row = lax.broadcasted_iota(jnp.int32, (1, 256), 1) < merged_starts[4]
        pos_ref[...] = jnp.where(live_row, own_row * 32 + rank, -1)

    key_pos = lax.broadcasted_iota(jnp.int32, (1, 1024), 1)
    segk = jnp.zeros((1, 1024), jnp.int32)
    for edge in starts[1:]:
        segk = segk + (key_pos >= edge).astype(jnp.int32)

    def project(slots, first=False):
        for half in (0, 1):
            where = [gq.slot(half, *s) for s in slots]

            def body(i, carry, half=half, where=where):
                out_cols = pl.ds(pl.multiple_of(i * 256, 256), 256)
                total = None
                for w in where:
                    cols = pl.ds(pl.multiple_of(w * 256, 256), 256)
                    term = dot(normed[:, cols], bufq[half, w, i])
                    total = term if total is None else total + term
                if first:
                    acc[half, :, out_cols] = total
                else:
                    acc[half, :, out_cols] += total
                return carry

            lax.fori_loop(0, 3, body, 0)

    for i in range(3):
        norm_chunk(i)
    for copy in own_q:
        copy.wait()
    gq.r2()
    norm_chunk(3)
    gq.r4a()
    project([(0, 0), (-1, 0), (1, 0)], first=True)
    project([(0, -1), (0, 1)])
    gq.r3()
    project([(2, 0)])
    lax.fori_loop(0, tiles, tables, 0)
    slots_layout()
    own_wo.wait()
    turned = wo_in[...].astype(F32).T.astype(BF16)
    for i in range(8):
        bufo[i, r] = turned[32 * i : 32 * i + 32, :]
    scale_own[...] = own_features(lambda cols: scale[:, cols])
    gain_own[...] = own_features(lambda cols: merge_gain[:, cols])
    bias_own[...] = own_features(lambda cols: merge_bias[:, cols])
    gq.r4b()
    go.r1()
    project([(-1, -1), (-1, 1), (1, -1), (1, 1)])
    gq.r4c()
    project([(2, -1), (2, 1)])
    gq.recv(12, 13, 14, 15)
    project([(0, 2), (-1, 2)])
    go.r2()
    go.r4a()
    gq.recv(16, 17, 18, 19)
    project([(1, 2), (2, 2)])
    go.r3()

    def rotate(i, carry):
        at = pl.ds(pl.multiple_of(i * rows_tile, rows_tile), rows_tile)
        cosine, sine = cos_ref[at, :], sin_ref[at, :]
        for head in range(4):
            half, inner = divmod(head, 2)
            for dst, base in ((qb, 0), (kb, 256)):
                v = acc[half, at, base + inner * 128 : base + inner * 128 + 128]
                partner = jnp.where(low, pltpu.roll(v, 96, 1), pltpu.roll(v, 32, 1))
                dst[at, head * 128 : head * 128 + 128] = (v * cosine + partner * sine).astype(BF16)
            vb[at, head * 128 : head * 128 + 128] = acc[
                half, at, 512 + inner * 128 : 512 + inner * 128 + 128
            ].astype(BF16)
        return carry

    lax.fori_loop(0, tiles, rotate, 0)

    factor = HEAD_DIM ** (-0.5) / math.log(2.0)

    def attend(k):
        at = slice(k * rows_tile, (k + 1) * rows_tile)
        pick = (
            lax.broadcasted_iota(jnp.int32, (rows_tile, 1024), 1) == src_ref[at, 0:1]
        ).astype(BF16)
        att[at, :] = dot(pick, qb[...]).astype(BF16)
        tokp[at, :] = dot(pick, tok[...]).astype(BF16)

        def body(head, carry):
            cols = pl.ds(pl.multiple_of(head * 128, 128), 128)
            s = lax.dot_general(
                att[at, cols], kb[:, cols], (((1,), (1,)), ((), ())), preferred_element_type=F32
            )
            s = jnp.where(segq_ref[:, 0:1] == segk, s, -jnp.inf)
            top = jnp.max(s, axis=-1, keepdims=True)
            e = jnp.exp2((s - top) * factor)
            total = jnp.sum(e, axis=-1, keepdims=True)
            o = dot(e.astype(BF16), vb[:, cols])
            att[at, cols] = (o / total).astype(BF16)
            return carry

        lax.fori_loop(0, 4, body, 0)

    def out_project(to):
        def body(j, carry):
            weight = bufo[to, pl.ds(j * 8, 8)].reshape(256, 512)
            total = lax.dot_general(
                att[...], weight, (((1,), (1,)), ((), ())), preferred_element_type=F32
            )
            cols = pl.ds(pl.multiple_of(to * 512 + j * 256, 256), 256)
            normed[:, cols] = total.astype(BF16)
            return carry

        lax.fori_loop(0, 2, body, 0)

    def chunk_of(tensor, lo=0, rows=1024):
        return normed.at[pl.ds(lo, rows), pl.ds(pl.multiple_of(tensor * 512, 512), 512)]

    def sib_copy(dz):
        return pltpu.make_async_remote_copy(
            src_ref=chunk_of(zdev(dz, 1 - c)),
            dst_ref=fromsib.at[dz % 4],
            send_sem=ssib.at[dz % 4],
            recv_sem=rsib.at[dz % 4],
            device_id=(r, sibling),
            device_id_type=MESH,
        )

    def opp_copy(which):
        return pltpu.make_async_remote_copy(
            src_ref=chunk_of(zdev(2), 512 * which, 512),
            dst_ref=(oppa, oppb)[which],
            send_sem=sopp.at[which],
            recv_sem=ropp.at[which],
            device_id=(r, zdev(1 if which == 0 else -1)),
            device_id_type=MESH,
        )

    def z_copy(which, part):
        to = zdev(1 if which == 0 else -1)
        return pltpu.make_async_remote_copy(
            src_ref=chunk_of(to, 512 * part, 512),
            dst_ref=(zprev, znext)[which].at[pl.ds(512 * part, 512)],
            send_sem=sz.at[which, part],
            recv_sem=rz.at[which, part],
            device_id=(r, to),
            device_id_type=MESH,
        )

    def to_sibling(dz):
        out_project(zdev(dz, 1 - c))
        sib_copy(dz).start()

    def to_own(dz):
        out_project(zdev(dz))

    def partial(dz):
        out_project(zdev(dz, 1 - c))
        sib_copy(dz).start()
        out_project(zdev(dz))

    def add_sibling(dz):
        sib_copy(dz).wait_recv()

        def body(i, carry):
            ref = chunk_of(zdev(dz), pl.multiple_of(i * 256, 256), 256)
            other = fromsib[dz % 4, pl.ds(pl.multiple_of(i * 256, 256), 256), :]
            ref[...] = (ref[...].astype(F32) + other.astype(F32)).astype(BF16)
            return carry

        lax.fori_loop(0, 4, body, 0)

    def pass_on(which):
        opp_copy(which).wait_recv()
        for i in (0, 1):
            ref = chunk_of(zdev(1 if which == 0 else -1), 512 * which + 256 * i, 256)
            other = (oppa, oppb)[which][256 * i : 256 * i + 256, :]
            ref[...] = (ref[...].astype(F32) + other.astype(F32)).astype(BF16)
        z_copy(which, which).start()

    sums = []

    def finish_rows(k):
        at = slice(k * rows_tile, (k + 1) * rows_tile)
        total = (
            chunk_of(t, k * rows_tile, rows_tile)[...].astype(F32)
            + fromsib[0, at, :].astype(F32)
            + zprev[at, :].astype(F32)
            + znext[at, :].astype(F32)
        )
        res = tokp[at, :].astype(F32) + scale_own[...] * total
        acc[0, at, 0:512] = res
        sums.append(jnp.sum(res, axis=-1, keepdims=True))

    go.r4b()
    attend(0)
    go.r4c()
    own_deal.wait()
    for step in range(1, 8):
        deal_wait(step)
    gm.r1()
    attend(1)
    attend(2)
    attend(3)
    go.finish()
    to_sibling(2)
    to_own(2)
    to_sibling(1)
    add_sibling(2)
    opp_copy(0).start()
    opp_copy(1).start()
    gm.r2()
    to_own(1)
    to_sibling(-1)
    add_sibling(1)
    z_copy(0, 1).start()
    gm.r4a()
    to_own(-1)
    to_sibling(0)
    add_sibling(-1)
    z_copy(1, 0).start()
    gm.r3()
    pass_on(0)
    pass_on(1)
    to_own(0)
    gm.r4b()
    gm.r4c()
    sib_copy(0).wait_recv()
    z_copy(0, 1).wait_recv()
    z_copy(1, 1).wait_recv()
    z_copy(0, 0).wait_recv()
    z_copy(1, 0).wait_recv()
    for k in range(4):
        finish_rows(k)

    mean_l = (sums[0] + sums[1] + sums[2] + sums[3]) * (1.0 / 2048)
    m2 = None
    for k in range(4):
        d = acc[0, k * 256 : (k + 1) * 256, 0:512] - mean_l
        term = jnp.sum(d * d, axis=-1, keepdims=True)
        m2 = term if m2 is None else m2 + term
    packed = jnp.where(lane == 0, mean_l, m2)
    stats[0] = packed.T[0:8, :]

    def stat_copy(step):
        return pltpu.make_async_remote_copy(
            src_ref=stats.at[0],
            dst_ref=stats.at[step],
            send_sem=sstat.at[step],
            recv_sem=rstat.at[step],
            device_id=(r, lax.rem(t + step, 8)),
            device_id_type=MESH,
        )

    for step in range(1, 8):
        stat_copy(step).start()
    gm.finish()
    for step in range(1, 8):
        stat_copy(step).wait_recv()
    means = [stats[i][0:1, :] for i in range(8)]
    m2s = [stats[i][1:2, :] for i in range(8)]
    mean = functools.reduce(lambda a, b: a + b, means) * 0.125
    total2 = functools.reduce(lambda a, b: a + b, m2s)
    for m in means:
        total2 = total2 + 2048.0 * (m - mean) * (m - mean)
    rs = lax.rsqrt(total2 * (1.0 / 16384) + 1e-6)
    row = lax.broadcasted_iota(jnp.int32, (128, 256), 0)
    back = jnp.where(row == 0, mean, rs).T
    mean_c, rs_c = back[:, 0:1], back[:, 1:2]
    for k in range(4):
        at = slice(k * rows_tile, (k + 1) * rows_tile)
        v = (acc[0, at, 0:512] - mean_c) * rs_c
        v = v * gain_own[k : k + 1, :] + bias_own[k : k + 1, :]
        att[at, :] = v.astype(BF16)

    def merge_chunk(core, dz):
        to = zdev(dz, core)
        cols = pl.ds(pl.multiple_of(to * 256, 256), 256)
        total = None
        for k in range(4):
            for j in (0, 1):
                term = dot(
                    att[k * 256 : (k + 1) * 256, j * 256 : j * 256 + 256],
                    bufm[k // 2, 8 * j : 8 * j + 8, k % 2, :, cols].reshape(256, 256),
                )
                total = term if total is None else total + term
        return total

    def msib_copy(dz):
        return pltpu.make_async_remote_copy(
            src_ref=mpart.at[1 - c, dz % 4],
            dst_ref=msib.at[dz % 4],
            send_sem=smsib.at[dz % 4],
            recv_sem=rmsib.at[dz % 4],
            device_id=(r, sibling),
            device_id_type=MESH,
        )

    def mopp_copy(which):
        return pltpu.make_async_remote_copy(
            src_ref=mpart.at[c, 2, pl.ds(128 * which, 128)],
            dst_ref=mopp.at[which],
            send_sem=smopp.at[which],
            recv_sem=rmopp.at[which],
            device_id=(r, zdev(1 if which == 0 else -1)),
            device_id_type=MESH,
        )

    def mz_copy(which, part):
        return pltpu.make_async_remote_copy(
            src_ref=mpart.at[c, 1 if which == 0 else 3, pl.ds(128 * part, 128)],
            dst_ref=mz.at[which, pl.ds(128 * part, 128)],
            send_sem=smz.at[which, part],
            recv_sem=rmz.at[which, part],
            device_id=(r, zdev(1 if which == 0 else -1)),
            device_id_type=MESH,
        )

    def merge_own(dz):
        total = merge_chunk(c, dz)
        msib_copy(dz).wait_recv()
        return total + msib[dz % 4].astype(F32)

    for dz in (2, 1, -1, 0):
        mpart[1 - c, dz % 4] = merge_chunk(1 - c, dz).astype(BF16)
        msib_copy(dz).start()
    mpart[c, 2] = merge_own(2).astype(BF16)
    for which in (0, 1):
        mopp_copy(which).start()
    mpart[c, 1] = merge_own(1).astype(BF16)
    mz_copy(0, 1).start()
    mpart[c, 3] = merge_own(-1).astype(BF16)
    mz_copy(1, 0).start()
    for which, index in ((0, 1), (1, 3)):
        mopp_copy(which).wait_recv()
        rows = pl.ds(128 * which, 128)
        mpart[c, index, rows, :] = (
            mpart[c, index, rows, :].astype(F32) + mopp[which].astype(F32)
        ).astype(BF16)
        mz_copy(which, which).start()
    merged = merge_own(0)
    for which in (0, 1):
        for part in (0, 1):
            mz_copy(which, part).wait_recv()
    merged = (merged + mz[0].astype(F32) + mz[1].astype(F32)).astype(BF16)

    place_row = (lax.broadcasted_iota(jnp.int32, (512, 256), 0) == pos_ref[...]).astype(BF16)
    obuf[...] = dot(place_row, merged).astype(BF16).reshape(16, 32, 256)

    def out_copy(step):
        to = lax.rem(r + step, 16)
        return pltpu.make_async_remote_copy(
            src_ref=obuf.at[to],
            dst_ref=out.at[r],
            send_sem=sout.at[step],
            recv_sem=rout.at[step],
            device_id=(to, t),
            device_id_type=MESH,
        )

    def out_wait(step):
        come = lax.rem(r + 16 - step, 16)
        pltpu.make_async_remote_copy(
            src_ref=obuf.at[come],
            dst_ref=out.at[come],
            send_sem=sout.at[step],
            recv_sem=rout.at[step],
            device_id=(come, t),
            device_id_type=MESH,
        ).wait_recv()

    own_out = pltpu.make_async_copy(obuf.at[r], out.at[r], local.at[9])
    for step in range(1, 16):
        out_copy(step).start()
    own_out.start()

    for step in range(1, 8):
        deal_copy(step).wait_send()
    for g in (gq, go, gm):
        g.drain()
    for dz in range(4):
        sib_copy(dz).wait_send()
    for which in (0, 1):
        opp_copy(which).wait_send()
        for part in (0, 1):
            z_copy(which, part).wait_send()
    for step in range(1, 8):
        stat_copy(step).wait_send()
    for dz in range(4):
        msib_copy(dz).wait_send()
    for which in (0, 1):
        mopp_copy(which).wait_send()
        for part in (0, 1):
            mz_copy(which, part).wait_send()
    own_out.wait()
    for step in range(1, 16):
        out_wait(step)
        out_copy(step).wait_send()


def per_device(
    tokens,
    grid_sizes,
    owners,
    ln_gain,
    ln_bias,
    w_qkv,
    w_out,
    layer_scale,
    merge_gain,
    merge_bias,
    w_merge,
):
    own_row = lax.dynamic_slice_in_dim(owners, lax.axis_index("rows") * 256, 256).reshape(1, 256)
    grid_row = lax.dynamic_slice_in_dim(grid_sizes, lax.axis_index("rows"), 1).reshape(1, 8)
    wq = w_qkv.transpose(1, 0, 2)
    wm = w_merge.reshape(2, 2, 256, 256)

    any_space = pl.BlockSpec(memory_space=pl.ANY)
    vmem = pl.BlockSpec(memory_space=pltpu.VMEM)
    dma = pltpu.SemaphoreType.DMA
    out = pl.pallas_call(
        kernel,
        out_shape=jax.ShapeDtypeStruct((16, 32, 256), BF16),
        in_specs=[any_space] * 4 + [vmem] * 7,
        out_specs=any_space,
        scratch_shapes=[
            pltpu.VMEM((2, 16, 3, 256, 256), BF16),
            pltpu.VMEM((8, 16, 32, 512), BF16),
            pltpu.VMEM((2, 16, 2, 32, 2048), BF16),
            pltpu.VMEM((1024, 4096), BF16),
            pltpu.VMEM((2, 1024, 768), F32),
            pltpu.VMEM((1024, 512), BF16),
            pltpu.VMEM((1024, 512), BF16),
            pltpu.VMEM((1024, 512), BF16),
            pltpu.VMEM((1024, 512), BF16),
            pltpu.VMEM((1024, 512), BF16),
            pltpu.VMEM((1024, 512), BF16),
            pltpu.VMEM((1024, 128), F32),
            pltpu.VMEM((1024, 128), F32),
            pltpu.VMEM((1024, 128), jnp.int32),
            pltpu.VMEM((256, 128), jnp.int32),
            pltpu.VMEM((1, 256), jnp.int32),
            pltpu.VMEM((512, 256), BF16),
            pltpu.VMEM((1, 512), F32),
            pltpu.VMEM((4, 512), F32),
            pltpu.VMEM((4, 512), F32),
            pltpu.VMEM((4, 1024, 512), BF16),
            pltpu.VMEM((512, 512), BF16),
            pltpu.VMEM((512, 512), BF16),
            pltpu.VMEM((1024, 512), BF16),
            pltpu.VMEM((1024, 512), BF16),
            pltpu.VMEM((8, 8, 256), F32),
            pltpu.VMEM((2, 4, 256, 256), BF16),
            pltpu.VMEM((4, 256, 256), BF16),
            pltpu.VMEM((2, 128, 256), BF16),
            pltpu.VMEM((2, 256, 256), BF16),
            pltpu.VMEM((16, 32, 256), BF16),
            dma((2, 20)),
            dma((2, 20)),
            dma((2, 20)),
            dma((2, 20)),
            dma((2, 20)),
            dma((2, 20)),
            dma((10,)),
            dma((8,)),
            dma((8,)),
            dma((4,)),
            dma((4,)),
            dma((2,)),
            dma((2,)),
            dma((2, 2)),
            dma((2, 2)),
            dma((8,)),
            dma((8,)),
            dma((4,)),
            dma((4,)),
            dma((2,)),
            dma((2,)),
            dma((2, 2)),
            dma((2, 2)),
            dma((16,)),
            dma((16,)),
        ],
        compiler_params=pltpu.CompilerParams(
            collective_id=0, has_side_effects=True, vmem_limit_bytes=63 * 2**20
        ),
    )(
        tokens,
        wq,
        w_out,
        wm,
        ln_gain[None],
        ln_bias[None],
        layer_scale[None],
        merge_gain,
        merge_bias,
        grid_row,
        own_row,
    )
    return out[:, :24].reshape(384, 256)


def solution(mesh):
    return jax.shard_map(
        per_device,
        mesh=mesh,
        in_specs=(
            P("rows", None),
            P(),
            P(),
            P(),
            P(),
            P("rows", None, "tensor"),
            P("tensor", "rows"),
            P(),
            P(),
            P(),
            P(None, "rows", "tensor"),
        ),
        out_specs=P("rows", "tensor"),
        check_vma=False,
    )
```

```python
import functools
import math

import jax
import jax.numpy as jnp
from jax import lax
from jax.experimental import pallas as pl
from jax.experimental.pallas import tpu as pltpu
from jax.sharding import PartitionSpec as P

MESH = pl.DeviceIdType.MESH
F32 = jnp.float32
BF16 = jnp.bfloat16
HEAD_DIM = 128
PREFIX = 5


class Gather:
    def __init__(self, src, region, send, recv, place):
        self.src, self.region, self.send, self.recv_sem = src, region, send, recv
        self.y, self.x, self.t = place
        table = [
            ((0, 0), None, (1, 0)),
            ((0, 0), None, (-1, 0)),
            ((0, 0), None, (0, 1)),
            ((0, 0), None, (0, -1)),
            ((-1, 0), 0, (1, 0)),
            ((1, 0), 1, (-1, 0)),
            ((-1, 0), None, (0, 1)),
            ((-1, 0), None, (0, -1)),
            ((1, 0), None, (0, 1)),
            ((1, 0), None, (0, -1)),
            ((2, 0), None, (0, 1)),
            ((2, 0), None, (0, -1)),
        ]
        for first in (0, -1, 1, 2):
            table.append(((first, -1), 0, (0, 1)))
            table.append(((first, 1), 1, (0, -1)))
        self.table = table

    def slot(self, half, first, second):
        dx, dy = (first, second) if half == 0 else (second, first)
        return lax.rem(self.y + (dy % 4), 4) * 4 + lax.rem(self.x + (dx % 4), 4)

    def copy(self, half, i):
        (first, second), part, to = self.table[i]
        slot = self.slot(half, first, second)
        dst = self.region(half, slot, part)
        src = self.src(half) if self.src is not None and i < 4 else dst
        return pltpu.make_async_remote_copy(
            src_ref=src,
            dst_ref=dst,
            send_sem=self.send.at[half, i],
            recv_sem=self.recv_sem.at[half, i],
            device_id=(self.slot(half, *to), self.t),
            device_id_type=MESH,
        )

    def start(self, *which):
        for i in which:
            for half in (0, 1):
                self.copy(half, i).start()

    def recv(self, *which):
        for i in which:
            for half in (0, 1):
                self.copy(half, i).wait_recv()

    def r1(self):
        self.start(0, 1, 2, 3)

    def r2(self):
        self.recv(0, 1)
        self.start(4, 5, 6, 7, 8, 9)

    def r3(self):
        self.recv(4, 5)
        self.start(10, 11)

    def r4a(self):
        self.recv(2, 3)
        self.start(12, 13)

    def r4b(self):
        self.recv(6, 7, 8, 9)
        self.start(14, 15, 16, 17)

    def r4c(self):
        self.recv(10, 11)
        self.start(18, 19)

    def finish(self):
        self.recv(12, 13, 14, 15, 16, 17, 18, 19)

    def drain(self):
        for i in range(20):
            for half in (0, 1):
                self.copy(half, i).wait_send()


def dot(a, b):
    return jnp.dot(a, b, preferred_element_type=F32)


def kernel(
    tokens,
    wq,
    wo,
    wm,
    ln_gain,
    ln_bias,
    scale,
    merge_gain,
    merge_bias,
    grid_ref,
    own_ref,
    out,
    bufq,
    bufo,
    bufm,
    normed,
    acc,
    qb,
    kb,
    vb,
    att,
    tok,
    tokp,
    cos_ref,
    sin_ref,
    src_ref,
    segq_ref,
    pos_ref,
    wo_in,
    scale_own,
    gain_own,
    bias_own,
    fromsib,
    oppa,
    oppb,
    zprev,
    znext,
    stats,
    mpart,
    msib,
    mopp,
    mz,
    obuf,
    sq,
    rq,
    so,
    ro,
    sm,
    rm,
    local,
    sperm,
    rperm,
    ssib,
    rsib,
    sopp,
    ropp,
    sz,
    rz,
    sstat,
    rstat,
    smsib,
    rmsib,
    smopp,
    rmopp,
    smz,
    rmz,
    sout,
    rout,
):
    r = lax.axis_index("rows")
    t = lax.axis_index("tensor")
    y, x = lax.div(r, 4), lax.rem(r, 4)
    z, c = lax.div(t, 2), lax.rem(t, 2)
    place = (y, x, t)
    tiles = 4
    rows_tile = 256

    def zdev(offset, core=None):
        return lax.rem(z + offset % 4, 4) * 2 + (c if core is None else core)

    sibling = z * 2 + (1 - c)
    barrier = pltpu.get_barrier_semaphore()
    for step in range(1, 16):
        pl.semaphore_signal(
            barrier, inc=1, device_id=(lax.rem(r + step, 16), t), device_id_type=MESH
        )
    for step in range(1, 8):
        pl.semaphore_signal(
            barrier, inc=1, device_id=(r, lax.rem(t + step, 8)), device_id_type=MESH
        )
    pl.semaphore_wait(barrier, 22)

    def src_q(half):
        return wq.at[:, :, pl.ds(256 * half, 256)]

    def region_q(half, slot, part):
        if part is None:
            return bufq.at[half, slot]
        return bufq.at[half, slot, :, pl.ds(128 * part, 128)]

    def region_o(half, slot, part):
        if part is None:
            return bufo.at[pl.ds(4 * half, 4), slot]
        return bufo.at[pl.ds(4 * half + 2 * part, 2), slot]

    def region_m(half, slot, part):
        return bufm.at[half, slot] if part is None else bufm.at[half, slot, part]

    gq = Gather(src_q, region_q, sq, rq, place)
    go = Gather(None, region_o, so, ro, place)
    gm = Gather(None, region_m, sm, rm, place)

    gq.r1()

    def deal_piece(to):
        return wm.at[:, :, pl.ds(pl.multiple_of(to * 32, 32), 32), :]

    def deal_place(come):
        return bufm.at[:, r, :, :, pl.ds(pl.multiple_of(come * 256, 256), 256)]

    def deal_copy(step):
        to = lax.rem(t + step, 8)
        return pltpu.make_async_remote_copy(
            src_ref=deal_piece(to),
            dst_ref=deal_place(t),
            send_sem=sperm.at[step],
            recv_sem=rperm.at[step],
            device_id=(r, to),
            device_id_type=MESH,
        )

    def deal_wait(step):
        come = lax.rem(t + 8 - step, 8)
        pltpu.make_async_remote_copy(
            src_ref=deal_piece(come),
            dst_ref=deal_place(come),
            send_sem=sperm.at[step],
            recv_sem=rperm.at[step],
            device_id=(r, come),
            device_id_type=MESH,
        ).wait_recv()

    own_deal = pltpu.make_async_copy(deal_piece(t), deal_place(t), local.at[6])

    chunk = 256

    def tok_copy(i):
        rows = pl.ds(i * chunk, chunk)
        return pltpu.make_async_copy(tokens.at[rows], normed.at[rows], local.at[i])

    for i in range(4):
        tok_copy(i).start()
    own_q = [pltpu.make_async_copy(src_q(h), bufq.at[h, r], local.at[4 + h]) for h in (0, 1)]
    own_wo = pltpu.make_async_copy(wo, wo_in, local.at[7])
    for copy in own_q + [own_wo, own_deal]:
        copy.start()
    for step in range(1, 8):
        deal_copy(step).start()

    feature_tile = lax.div(t, 4) * 128

    def own_features(load):
        tiles_out = []
        for j in range(4):
            taken = None
            for q in range(4):
                v = load(pl.ds(pl.multiple_of(256 * (4 * j + q) + feature_tile, 128), 128))
                v = pltpu.roll(v, lax.rem(32 * q + 128 - 32 * lax.rem(t, 4), 128), 1)
                if q:
                    at = lax.broadcasted_iota(jnp.int32, v.shape, 1)
                    v = jnp.where(at >= 32 * q, v, taken)
                taken = v
            tiles_out.append(taken)
        return jnp.concatenate(tiles_out, axis=1)

    def norm_chunk(i):
        tok_copy(i).wait()
        step = 16

        def body(j, carry):
            at = pl.ds(pl.multiple_of(i * chunk + j * step, step), step)
            tok[at, :] = own_features(lambda cols: normed[at, cols].astype(F32)).astype(BF16)
            v = normed[at, :].astype(F32)
            mean = jnp.mean(v, axis=-1, keepdims=True)
            v = v - mean
            var = jnp.mean(v * v, axis=-1, keepdims=True)
            v = v * lax.rsqrt(var + 1e-6) * ln_gain[...] + ln_bias[...]
            normed[at, :] = v.astype(BF16)
            return carry

        lax.fori_loop(0, chunk // step, body, 0)

    grid = grid_ref[...]
    heights = [grid[:, 2 * i : 2 * i + 1] for i in range(4)]
    widths = [grid[:, 2 * i + 1 : 2 * i + 2] for i in range(4)]
    starts, merged_starts = [jnp.zeros((1, 1), jnp.int32)], [jnp.zeros((1, 1), jnp.int32)]
    for h, w in zip(heights, widths):
        starts.append(starts[-1] + PREFIX + h * w)
        merged_starts.append(merged_starts[-1] + ((h * w).astype(F32) * 0.25).astype(jnp.int32))
    lane = lax.broadcasted_iota(jnp.int32, (rows_tile, HEAD_DIM), 1)
    low = lax.rem(lane, 64) < 32

    freqs = jnp.exp2(lax.rem(lane[0:1, :], 32).astype(F32) * (-math.log2(100.0) / 32))

    def choose(at, edges, values):
        chosen = jnp.zeros(at.shape, jnp.int32) + values[0]
        for edge, value in zip(edges[1:4], values[1:4]):
            chosen = jnp.where(at >= edge, value, chosen)
        return chosen

    def tables(i, carry):
        at = pl.ds(pl.multiple_of(i * rows_tile, rows_tile), rows_tile)
        pos = lax.broadcasted_iota(jnp.int32, (rows_tile, HEAD_DIM), 0) + i * rows_tile
        local_pos = pos - choose(pos, starts, starts) - PREFIX
        patch = (local_pos >= 0) & (pos < starts[4])
        flat = jnp.where(patch, local_pos, 0).astype(F32)
        width = choose(pos, starts, widths).astype(F32)
        row = jnp.floor((flat + 0.5) / width)
        angle = jnp.where(lane < 64, row, flat - row * width) * freqs
        cos_ref[at, :] = jnp.cos(angle)
        sine = jnp.sin(angle)
        sin_ref[at, :] = jnp.where(low, -sine, sine)
        return carry

    def slots_layout():
        m = lax.broadcasted_iota(jnp.int32, (rows_tile, HEAD_DIM), 0)
        live = m < merged_starts[4]
        width = choose(m, merged_starts, widths).astype(F32)
        first = choose(m, merged_starts, starts).astype(F32) + PREFIX
        offset = (m - choose(m, merged_starts, merged_starts)).astype(F32)
        row = jnp.floor((offset + 0.5) / (0.5 * width))
        corner = first + (2.0 * row) * width + 2.0 * (offset - row * (0.5 * width))
        for k in range(4):
            source = corner + width * float(k // 2) + float(k % 2)
            src_ref[k * rows_tile : (k + 1) * rows_tile, :] = jnp.where(live, source, 0.0).astype(
                jnp.int32
            )
        segq_ref[...] = jnp.where(live, choose(m, merged_starts, [0, 1, 2, 3]), 0)

        own_row = own_ref[...]
        own_col = jnp.broadcast_to(own_row.astype(F32), (HEAD_DIM, 256)).T[:, 0:1]
        before = lax.broadcasted_iota(jnp.int32, (256, 256), 0) < lax.broadcasted_iota(
            jnp.int32, (256, 256), 1
        )
        hit = before & (own_col == own_row.astype(F32))
        rank = jnp.sum(jnp.where(hit, 1.0, 0.0), axis=0, keepdims=True).astype(jnp.int32)
        live_row = lax.broadcasted_iota(jnp.int32, (1, 256), 1) < merged_starts[4]
        pos_ref[...] = jnp.where(live_row, own_row * 32 + rank, -1)

    key_pos = lax.broadcasted_iota(jnp.int32, (1, 1024), 1)
    segk = jnp.zeros((1, 1024), jnp.int32)
    for edge in starts[1:]:
        segk = segk + (key_pos >= edge).astype(jnp.int32)

    def project(slots, first=False):
        for half in (0, 1):
            where = [gq.slot(half, *s) for s in slots]

            def body(i, carry, half=half, where=where):
                out_cols = pl.ds(pl.multiple_of(i * 256, 256), 256)
                total = None
                for w in where:
                    cols = pl.ds(pl.multiple_of(w * 256, 256), 256)
                    term = dot(normed[:, cols], bufq[half, w, i])
                    total = term if total is None else total + term
                if first:
                    acc[half, :, out_cols] = total
                else:
                    acc[half, :, out_cols] += total
                return carry

            lax.fori_loop(0, 3, body, 0)

    for i in range(3):
        norm_chunk(i)
    for copy in own_q:
        copy.wait()
    gq.r2()
    norm_chunk(3)
    gq.r4a()
    project([(0, 0), (-1, 0), (1, 0)], first=True)
    project([(0, -1), (0, 1)])
    gq.r3()
    project([(2, 0)])
    lax.fori_loop(0, tiles, tables, 0)
    slots_layout()
    own_wo.wait()
    turned = wo_in[...].astype(F32).T.astype(BF16)
    for i in range(8):
        bufo[i, r] = turned[32 * i : 32 * i + 32, :]
    scale_own[...] = own_features(lambda cols: scale[:, cols])
    gain_own[...] = own_features(lambda cols: merge_gain[:, cols])
    bias_own[...] = own_features(lambda cols: merge_bias[:, cols])
    gq.r4b()
    go.r1()
    project([(-1, -1), (-1, 1), (1, -1), (1, 1)])
    gq.r4c()
    project([(2, -1), (2, 1)])
    gq.recv(12, 13, 14, 15)
    project([(0, 2), (-1, 2)])
    go.r2()
    go.r4a()
    gq.recv(16, 17, 18, 19)
    project([(1, 2), (2, 2)])
    go.r3()

    def rotate(i, carry):
        at = pl.ds(pl.multiple_of(i * rows_tile, rows_tile), rows_tile)
        cosine, sine = cos_ref[at, :], sin_ref[at, :]
        for head in range(4):
            half, inner = divmod(head, 2)
            for dst, base in ((qb, 0), (kb, 256)):
                v = acc[half, at, base + inner * 128 : base + inner * 128 + 128]
                partner = jnp.where(low, pltpu.roll(v, 96, 1), pltpu.roll(v, 32, 1))
                dst[at, head * 128 : head * 128 + 128] = (v * cosine + partner * sine).astype(BF16)
            vb[at, head * 128 : head * 128 + 128] = acc[
                half, at, 512 + inner * 128 : 512 + inner * 128 + 128
            ].astype(BF16)
        return carry

    lax.fori_loop(0, tiles, rotate, 0)

    factor = HEAD_DIM ** (-0.5) / math.log(2.0)

    def attend(k):
        at = slice(k * rows_tile, (k + 1) * rows_tile)
        pick = (
            lax.broadcasted_iota(jnp.int32, (rows_tile, 1024), 1) == src_ref[at, 0:1]
        ).astype(BF16)
        att[at, :] = dot(pick, qb[...]).astype(BF16)
        tokp[at, :] = dot(pick, tok[...]).astype(BF16)

        def body(head, carry):
            cols = pl.ds(pl.multiple_of(head * 128, 128), 128)
            s = lax.dot_general(
                att[at, cols], kb[:, cols], (((1,), (1,)), ((), ())), preferred_element_type=F32
            )
            s = jnp.where(segq_ref[:, 0:1] == segk, s, -jnp.inf)
            top = jnp.max(s, axis=-1, keepdims=True)
            e = jnp.exp2((s - top) * factor)
            total = jnp.sum(e, axis=-1, keepdims=True)
            o = dot(e.astype(BF16), vb[:, cols])
            att[at, cols] = (o / total).astype(BF16)
            return carry

        lax.fori_loop(0, 4, body, 0)

    def out_project(to, lo=0, rows=1024):
        def body(j, carry):
            weight = bufo[to, pl.ds(j * 8, 8)].reshape(256, 512)
            total = lax.dot_general(
                att[lo : lo + rows, :], weight, (((1,), (1,)), ((), ())), preferred_element_type=F32
            )
            cols = pl.ds(pl.multiple_of(to * 512 + j * 256, 256), 256)
            normed[lo : lo + rows, cols] = total.astype(BF16)
            return carry

        lax.fori_loop(0, 2, body, 0)

    def chunk_of(tensor, lo=0, rows=1024):
        return normed.at[pl.ds(lo, rows), pl.ds(pl.multiple_of(tensor * 512, 512), 512)]

    def sib_copy(dz):
        return pltpu.make_async_remote_copy(
            src_ref=chunk_of(zdev(dz, 1 - c)),
            dst_ref=fromsib.at[dz % 4],
            send_sem=ssib.at[dz % 4],
            recv_sem=rsib.at[dz % 4],
            device_id=(r, sibling),
            device_id_type=MESH,
        )

    def sib_half(part):
        return pltpu.make_async_remote_copy(
            src_ref=chunk_of(zdev(2, 1 - c), 512 * part, 512),
            dst_ref=fromsib.at[2, pl.ds(512 * part, 512)],
            send_sem=ssib.at[2 + 2 * part],
            recv_sem=rsib.at[2 + 2 * part],
            device_id=(r, sibling),
            device_id_type=MESH,
        )

    def opp_copy(which):
        return pltpu.make_async_remote_copy(
            src_ref=chunk_of(zdev(2), 512 * which, 512),
            dst_ref=(oppa, oppb)[which],
            send_sem=sopp.at[which],
            recv_sem=ropp.at[which],
            device_id=(r, zdev(1 if which == 0 else -1)),
            device_id_type=MESH,
        )

    def z_copy(which, part):
        to = zdev(1 if which == 0 else -1)
        return pltpu.make_async_remote_copy(
            src_ref=chunk_of(to, 512 * part, 512),
            dst_ref=(zprev, znext)[which].at[pl.ds(512 * part, 512)],
            send_sem=sz.at[which, part],
            recv_sem=rz.at[which, part],
            device_id=(r, to),
            device_id_type=MESH,
        )

    def to_sibling(dz):
        out_project(zdev(dz, 1 - c))
        sib_copy(dz).start()

    def to_own(dz):
        out_project(zdev(dz))

    def add_sibling(dz):
        sib_copy(dz).wait_recv()

        def body(i, carry):
            ref = chunk_of(zdev(dz), pl.multiple_of(i * 256, 256), 256)
            other = fromsib[dz % 4, pl.ds(pl.multiple_of(i * 256, 256), 256), :]
            ref[...] = (ref[...].astype(F32) + other.astype(F32)).astype(BF16)
            return carry

        lax.fori_loop(0, 4, body, 0)

    def pass_on(which):
        opp_copy(which).wait_recv()
        for i in (0, 1):
            ref = chunk_of(zdev(1 if which == 0 else -1), 512 * which + 256 * i, 256)
            other = (oppa, oppb)[which][256 * i : 256 * i + 256, :]
            ref[...] = (ref[...].astype(F32) + other.astype(F32)).astype(BF16)
        z_copy(which, which).start()

    sums = []

    def begin_rows(k):
        at = slice(k * rows_tile, (k + 1) * rows_tile)
        total = (
            chunk_of(t, k * rows_tile, rows_tile)[...].astype(F32)
            + fromsib[0, at, :].astype(F32)
            + (znext if k < 2 else zprev)[at, :].astype(F32)
        )
        acc[0, at, 0:512] = tokp[at, :].astype(F32) + scale_own[...] * total

    def finish_rows(k):
        at = slice(k * rows_tile, (k + 1) * rows_tile)
        late = (zprev if k < 2 else znext)[at, :].astype(F32)
        res = acc[0, at, 0:512] + scale_own[...] * late
        acc[0, at, 0:512] = res
        sums.append(jnp.sum(res, axis=-1, keepdims=True))

    go.r4b()
    attend(0)
    go.r4c()
    own_deal.wait()
    for step in range(1, 8):
        deal_wait(step)
    gm.r1()
    attend(1)
    attend(2)
    attend(3)
    go.finish()
    for part in (0, 1):
        out_project(zdev(2, 1 - c), 512 * part, 512)
        sib_half(part).start()
    for part in (0, 1):
        out_project(zdev(2), 512 * part, 512)
        sib_half(part).wait_recv()
        for i in (0, 1):
            lo = 512 * part + 256 * i
            ref = chunk_of(zdev(2), lo, 256)
            other = fromsib[2, lo : lo + 256, :]
            ref[...] = (ref[...].astype(F32) + other.astype(F32)).astype(BF16)
        opp_copy(part).start()
    to_sibling(1)
    gm.r2()
    to_own(1)
    to_sibling(-1)
    add_sibling(1)
    z_copy(0, 1).start()
    gm.r4a()
    to_own(-1)
    to_sibling(0)
    add_sibling(-1)
    z_copy(1, 0).start()
    gm.r3()
    pass_on(0)
    pass_on(1)
    to_own(0)
    gm.r4b()
    gm.r4c()
    gq.drain()
    go.drain()
    sib_copy(0).wait_recv()
    z_copy(0, 1).wait_recv()
    z_copy(1, 0).wait_recv()
    for k in range(4):
        begin_rows(k)
    z_copy(0, 0).wait_recv()
    z_copy(1, 1).wait_recv()
    for k in range(4):
        finish_rows(k)

    mean_l = (sums[0] + sums[1] + sums[2] + sums[3]) * (1.0 / 2048)
    m2 = None
    for k in range(4):
        d = acc[0, k * 256 : (k + 1) * 256, 0:512] - mean_l
        term = jnp.sum(d * d, axis=-1, keepdims=True)
        m2 = term if m2 is None else m2 + term
    packed = jnp.where(lane == 0, mean_l, m2)
    stats[0] = packed.T[0:8, :]

    def stat_copy(step):
        return pltpu.make_async_remote_copy(
            src_ref=stats.at[0],
            dst_ref=stats.at[step],
            send_sem=sstat.at[step],
            recv_sem=rstat.at[step],
            device_id=(r, lax.rem(t + step, 8)),
            device_id_type=MESH,
        )

    for step in range(1, 8):
        stat_copy(step).start()
    gm.finish()
    gm.drain()
    for step in range(1, 8):
        stat_copy(step).wait_recv()
    means = [stats[i][0:1, :] for i in range(8)]
    m2s = [stats[i][1:2, :] for i in range(8)]
    mean = functools.reduce(lambda a, b: a + b, means) * 0.125
    total2 = functools.reduce(lambda a, b: a + b, m2s)
    for m in means:
        total2 = total2 + 2048.0 * (m - mean) * (m - mean)
    rs = lax.rsqrt(total2 * (1.0 / 16384) + 1e-6)
    row = lax.broadcasted_iota(jnp.int32, (128, 256), 0)
    back = jnp.where(row == 0, mean, rs).T
    mean_c, rs_c = back[:, 0:1], back[:, 1:2]
    for k in range(4):
        at = slice(k * rows_tile, (k + 1) * rows_tile)
        v = (acc[0, at, 0:512] - mean_c) * rs_c
        v = v * gain_own[k : k + 1, :] + bias_own[k : k + 1, :]
        att[at, :] = v.astype(BF16)

    def merge_chunk(core, dz):
        to = zdev(dz, core)
        cols = pl.ds(pl.multiple_of(to * 256, 256), 256)
        total = None
        for k in range(4):
            for j in (0, 1):
                term = dot(
                    att[k * 256 : (k + 1) * 256, j * 256 : j * 256 + 256],
                    bufm[k // 2, 8 * j : 8 * j + 8, k % 2, :, cols].reshape(256, 256),
                )
                total = term if total is None else total + term
        return total

    def msib_copy(dz):
        return pltpu.make_async_remote_copy(
            src_ref=mpart.at[1 - c, dz % 4],
            dst_ref=msib.at[dz % 4],
            send_sem=smsib.at[dz % 4],
            recv_sem=rmsib.at[dz % 4],
            device_id=(r, sibling),
            device_id_type=MESH,
        )

    def mopp_copy(which):
        return pltpu.make_async_remote_copy(
            src_ref=mpart.at[c, 2, pl.ds(128 * which, 128)],
            dst_ref=mopp.at[which],
            send_sem=smopp.at[which],
            recv_sem=rmopp.at[which],
            device_id=(r, zdev(1 if which == 0 else -1)),
            device_id_type=MESH,
        )

    def mz_copy(which, part):
        return pltpu.make_async_remote_copy(
            src_ref=mpart.at[c, 1 if which == 0 else 3, pl.ds(128 * part, 128)],
            dst_ref=mz.at[which, pl.ds(128 * part, 128)],
            send_sem=smz.at[which, part],
            recv_sem=rmz.at[which, part],
            device_id=(r, zdev(1 if which == 0 else -1)),
            device_id_type=MESH,
        )

    def merge_own(dz):
        total = merge_chunk(c, dz)
        msib_copy(dz).wait_recv()
        return total + msib[dz % 4].astype(F32)

    for dz in (2, 1, -1, 0):
        mpart[1 - c, dz % 4] = merge_chunk(1 - c, dz).astype(BF16)
        msib_copy(dz).start()
    mpart[c, 2] = merge_own(2).astype(BF16)
    for which in (0, 1):
        mopp_copy(which).start()
    mpart[c, 1] = merge_own(1).astype(BF16)
    mz_copy(0, 1).start()
    mpart[c, 3] = merge_own(-1).astype(BF16)
    mz_copy(1, 0).start()
    for which, index in ((0, 1), (1, 3)):
        mopp_copy(which).wait_recv()
        rows = pl.ds(128 * which, 128)
        mpart[c, index, rows, :] = (
            mpart[c, index, rows, :].astype(F32) + mopp[which].astype(F32)
        ).astype(BF16)
        mz_copy(which, which).start()
    merged = merge_own(0)
    for which in (0, 1):
        for part in (0, 1):
            mz_copy(which, part).wait_recv()
    merged = (merged + mz[0].astype(F32) + mz[1].astype(F32)).astype(BF16)

    place_row = (lax.broadcasted_iota(jnp.int32, (512, 256), 0) == pos_ref[...]).astype(BF16)
    obuf[...] = dot(place_row, merged).astype(BF16).reshape(16, 32, 256)

    def out_copy(step):
        to = lax.rem(r + step, 16)
        return pltpu.make_async_remote_copy(
            src_ref=obuf.at[to],
            dst_ref=out.at[r],
            send_sem=sout.at[step],
            recv_sem=rout.at[step],
            device_id=(to, t),
            device_id_type=MESH,
        )

    def out_wait(step):
        come = lax.rem(r + 16 - step, 16)
        pltpu.make_async_remote_copy(
            src_ref=obuf.at[come],
            dst_ref=out.at[come],
            send_sem=sout.at[step],
            recv_sem=rout.at[step],
            device_id=(come, t),
            device_id_type=MESH,
        ).wait_recv()

    own_out = pltpu.make_async_copy(obuf.at[r], out.at[r], local.at[9])
    for step in range(1, 16):
        out_copy(step).start()
    own_out.start()

    for step in range(1, 8):
        deal_copy(step).wait_send()
    for dz in (0, 1, 3):
        sib_copy(dz).wait_send()
    for part in (0, 1):
        sib_half(part).wait_send()
    for which in (0, 1):
        opp_copy(which).wait_send()
        for part in (0, 1):
            z_copy(which, part).wait_send()
    for step in range(1, 8):
        stat_copy(step).wait_send()
    for dz in range(4):
        msib_copy(dz).wait_send()
    for which in (0, 1):
        mopp_copy(which).wait_send()
        for part in (0, 1):
            mz_copy(which, part).wait_send()
    own_out.wait()
    for step in range(1, 16):
        out_wait(step)
        out_copy(step).wait_send()


def per_device(
    tokens,
    grid_sizes,
    owners,
    ln_gain,
    ln_bias,
    w_qkv,
    w_out,
    layer_scale,
    merge_gain,
    merge_bias,
    w_merge,
):
    own_row = lax.dynamic_slice_in_dim(owners, lax.axis_index("rows") * 256, 256).reshape(1, 256)
    grid_row = lax.dynamic_slice_in_dim(grid_sizes, lax.axis_index("rows"), 1).reshape(1, 8)
    wq = w_qkv.transpose(1, 0, 2)
    wm = w_merge.reshape(2, 2, 256, 256)

    any_space = pl.BlockSpec(memory_space=pl.ANY)
    vmem = pl.BlockSpec(memory_space=pltpu.VMEM)
    dma = pltpu.SemaphoreType.DMA
    out = pl.pallas_call(
        kernel,
        out_shape=jax.ShapeDtypeStruct((16, 32, 256), BF16),
        in_specs=[any_space] * 4 + [vmem] * 7,
        out_specs=any_space,
        scratch_shapes=[
            pltpu.VMEM((2, 16, 3, 256, 256), BF16),
            pltpu.VMEM((8, 16, 32, 512), BF16),
            pltpu.VMEM((2, 16, 2, 32, 2048), BF16),
            pltpu.VMEM((1024, 4096), BF16),
            pltpu.VMEM((2, 1024, 768), F32),
            pltpu.VMEM((1024, 512), BF16),
            pltpu.VMEM((1024, 512), BF16),
            pltpu.VMEM((1024, 512), BF16),
            pltpu.VMEM((1024, 512), BF16),
            pltpu.VMEM((1024, 512), BF16),
            pltpu.VMEM((1024, 512), BF16),
            pltpu.VMEM((1024, 128), F32),
            pltpu.VMEM((1024, 128), F32),
            pltpu.VMEM((1024, 128), jnp.int32),
            pltpu.VMEM((256, 128), jnp.int32),
            pltpu.VMEM((1, 256), jnp.int32),
            pltpu.VMEM((512, 256), BF16),
            pltpu.VMEM((1, 512), F32),
            pltpu.VMEM((4, 512), F32),
            pltpu.VMEM((4, 512), F32),
            pltpu.VMEM((4, 1024, 512), BF16),
            pltpu.VMEM((512, 512), BF16),
            pltpu.VMEM((512, 512), BF16),
            pltpu.VMEM((1024, 512), BF16),
            pltpu.VMEM((1024, 512), BF16),
            pltpu.VMEM((8, 8, 256), F32),
            pltpu.VMEM((2, 4, 256, 256), BF16),
            pltpu.VMEM((4, 256, 256), BF16),
            pltpu.VMEM((2, 128, 256), BF16),
            pltpu.VMEM((2, 256, 256), BF16),
            pltpu.VMEM((16, 32, 256), BF16),
            dma((2, 20)),
            dma((2, 20)),
            dma((2, 20)),
            dma((2, 20)),
            dma((2, 20)),
            dma((2, 20)),
            dma((10,)),
            dma((8,)),
            dma((8,)),
            dma((5,)),
            dma((5,)),
            dma((2,)),
            dma((2,)),
            dma((2, 2)),
            dma((2, 2)),
            dma((8,)),
            dma((8,)),
            dma((4,)),
            dma((4,)),
            dma((2,)),
            dma((2,)),
            dma((2, 2)),
            dma((2, 2)),
            dma((16,)),
            dma((16,)),
        ],
        compiler_params=pltpu.CompilerParams(
            collective_id=0, has_side_effects=True, vmem_limit_bytes=63 * 2**20
        ),
    )(
        tokens,
        wq,
        w_out,
        wm,
        ln_gain[None],
        ln_bias[None],
        layer_scale[None],
        merge_gain,
        merge_bias,
        grid_row,
        own_row,
    )
    return out[:, :24].reshape(384, 256)


def solution(mesh):
    return jax.shard_map(
        per_device,
        mesh=mesh,
        in_specs=(
            P("rows", None),
            P(),
            P(),
            P(),
            P(),
            P("rows", None, "tensor"),
            P("tensor", "rows"),
            P(),
            P(),
            P(),
            P(None, "rows", "tensor"),
        ),
        out_specs=P("rows", "tensor"),
        check_vma=False,
    )
```
